256 devices in a mesh: head: 8 (over z_hi, core), blk: 32 (over z_lo, x, y).
Axes of the slice: x: 4, y: 4, z: 8 (z_hi: 4, z_lo: 2; z = z_hi * 2 + z_lo), core: 2. Of those that a mesh axis runs over, the one named last changes fastest.
Arguments:
- queries: bfloat16 [32, 512, 2048], P('blk', 'head'), may hold values from -10 to 10
- keys: bfloat16 [32, 512, 512], P('blk', 'head'), may hold values from -10 to 10
- values: bfloat16 [32, 512, 512], P('blk', 'head'), may hold values from -6 to 6
- position: int32 [32, 512], replicated, may hold values from 0 to 16383, as said below
- segment: int32 [32, 512], replicated, may hold values from 0 to 3, as said below
Outputs:
- attended: bfloat16 [32, 512, 2048], P('blk', 'head')
The draws below stay inside these ranges and needn't reach their ends.
Inputs may be any that keep to these rules, and one draw needn't show every extreme that they name: Each row b holds two runs of 256 consecutive positions in rising order, first c * 256 onward, then (63 - c) * 256 onward, with c a permutation of the rows; every position appears once. `segment`: documents are runs of consecutive positions; their numbers rise with position, start at 0 and may skip values.
All inputs are finite; a program needn't handle non-finite values.
Results may differ from the reference program's by a relative error of at most 0.007.
Values may be sent and summed in bfloat16 or wider, within the bound.
No kernel may reach another device: no remote copies, remote signals or barrier semaphores. Data moves between devices by JAX's collectives and lax.ppermute only.
A program may use at most 128 MiB of HBM per device.

```python
import jax
import jax.numpy as jnp
from jax import lax

LOCAL_QUERY_HEADS = 16
LOCAL_KV_HEADS = 4
HEAD_SIZE = 128
TOKENS_PER_BLOCK = 512
STORED_BLOCKS = 32
SEQUENCE_TOKENS = 16384


def zig_layout(key):
    base = jax.random.fold_in(key, 200)
    order = jax.random.permutation(base, STORED_BLOCKS).astype(jnp.int32)
    half = TOKENS_PER_BLOCK // 2
    within = jnp.arange(half, dtype=jnp.int32)
    lower = order[:, None] * half + within[None, :]
    upper = (2 * STORED_BLOCKS - 1 - order)[:, None] * half + within[None, :]
    return jnp.concatenate([lower, upper], axis=1).astype(jnp.int32)


def draw_queries(key, part):
    key = jax.random.fold_in(key, 1)
    attention_result = jax.random.truncated_normal(key, -4.0, 4.0, (STORED_BLOCKS, TOKENS_PER_BLOCK, LOCAL_QUERY_HEADS, HEAD_SIZE), jnp.float32)
    return attention_result.reshape(STORED_BLOCKS, TOKENS_PER_BLOCK, LOCAL_QUERY_HEADS * HEAD_SIZE).astype(jnp.bfloat16)


def draw_keys(key, part):
    key = jax.random.fold_in(key, 2)
    attention_result = jax.random.truncated_normal(key, -4.0, 4.0, (STORED_BLOCKS, TOKENS_PER_BLOCK, LOCAL_KV_HEADS, HEAD_SIZE), jnp.float32)
    return attention_result.reshape(STORED_BLOCKS, TOKENS_PER_BLOCK, LOCAL_KV_HEADS * HEAD_SIZE).astype(jnp.bfloat16)


def draw_position(key, part):
    return zig_layout(key)


def draw_segment(key, part):
    placed = zig_layout(key)
    key = jax.random.fold_in(key, 7)
    bounds = jax.random.randint(key, (3,), 1, STORED_BLOCKS * TOKENS_PER_BLOCK).astype(jnp.int32)
    return jnp.sum((placed[:, :, None] >= bounds[None, None, :]).astype(jnp.int32), axis=-1).astype(jnp.int32)


def steps_of(key, extent, cuts, least, high):
    def one(axis_at, blocks):
        heights = jax.random.uniform(jax.random.fold_in(jax.random.fold_in(key, 6), axis_at), (blocks,), jnp.float32, least / len(cuts), high / len(cuts))
        return jnp.repeat(jnp.exp(heights), extent[axis_at] // blocks).reshape((-1,) + (1,) * (len(extent) - axis_at - 1))

    level = one(*cuts[0])
    for cut in cuts[1:]:
        level = level * one(*cut)
    return level


def scatter_about(stream_key, shape, spread, limit, cuts=(), kind=jnp.bfloat16):
    result = spread * jax.random.normal(stream_key, shape, jnp.float32)
    if cuts:
        result = result * steps_of(stream_key, shape, cuts, -0.22, 0.18)
    return jnp.clip(result, -limit, limit).astype(kind)


def setup_inputs(seed: int = 0) -> dict:
    key_list = jax.random.split(jax.random.key(seed), 6)
    return {
        "queries": draw_queries(jax.random.fold_in(key_list[5], 71), 0),
        "keys": draw_keys(jax.random.fold_in(key_list[5], 71), 0),
        "values": scatter_about(key_list[2], (STORED_BLOCKS, TOKENS_PER_BLOCK, LOCAL_KV_HEADS * HEAD_SIZE), 1.0, 6.0, ((0, 32), (1, 8))),
        "position": draw_position(jax.random.fold_in(key_list[5], 71), 0),
        "segment": draw_segment(jax.random.fold_in(key_list[5], 71), 0),
    }


masked_score = -1.0e30


def attend_block(block, gathered_keys, gathered_values, pos_all, seg_all):
    queries_blk, pos_blk, seg_blk = block
    visible = (seg_all[None, :] == seg_blk[:, None]) & (pos_all[None, :] <= pos_blk[:, None])
    query_group = LOCAL_QUERY_HEADS // LOCAL_KV_HEADS
    pieces = []
    for shared_kv_head in range(LOCAL_KV_HEADS):
        query_part = queries_blk[:, shared_kv_head * query_group:(shared_kv_head + 1) * query_group, :].astype(jnp.float32)
        key_part = gathered_keys[:, shared_kv_head, :].astype(jnp.float32)
        scores = jnp.einsum("tgd,sd->gts", query_part, key_part) * (HEAD_SIZE ** -0.5)
        scores = jnp.where(visible[None], scores, masked_score)
        row_top = jnp.max(scores, axis=-1, keepdims=True)
        weights = jnp.where(visible[None], jnp.exp(scores - row_top), 0.0)
        totals = jnp.sum(weights, axis=-1)
        rounded = lax.optimization_barrier(weights.astype(jnp.bfloat16)).astype(jnp.float32)
        context = jnp.einsum("gts,sd->tgd", rounded, gathered_values[:, shared_kv_head, :].astype(jnp.float32))
        pieces.append(context / jnp.transpose(totals)[:, :, None])
    joined = jnp.concatenate(pieces, axis=1)
    return joined.reshape(TOKENS_PER_BLOCK, LOCAL_QUERY_HEADS * HEAD_SIZE).astype(jnp.bfloat16)


def reference(queries, keys, values, position, segment):
    query_heads = queries.reshape(STORED_BLOCKS, TOKENS_PER_BLOCK, LOCAL_QUERY_HEADS, HEAD_SIZE)
    gathered_keys = keys.reshape(SEQUENCE_TOKENS, LOCAL_KV_HEADS, HEAD_SIZE)
    gathered_values = values.reshape(SEQUENCE_TOKENS, LOCAL_KV_HEADS, HEAD_SIZE)
    pos_all = position.reshape(SEQUENCE_TOKENS)
    seg_all = segment.reshape(SEQUENCE_TOKENS)

    def one_block(block):
        return attend_block(block, gathered_keys, gathered_values, pos_all, seg_all)

    return lax.map(one_block, (query_heads, position, segment))
```

```python
import functools

import jax
import jax.numpy as jnp
import numpy as np
from jax import lax
from jax.experimental import pallas as pl
from jax.experimental.pallas import tpu as pltpu
from jax.sharding import PartitionSpec as P

HEADS = 16
KV = 4
D = 128
AXES = ("head", "blk")
NEVER = 1 << 20
MASKED = -1e30
LOG2E_SCALE = float(np.log2(np.e) * D**-0.5)
VMEM_LIMIT = 40 * 1024 * 1024


def device_of(zl, x, y, zh, c):
    return ((zh % 4) * 2 + c % 2) * 32 + (zl % 2) * 16 + (x % 4) * 4 + y % 4


def place_of(device):
    h, b = device // 32, device % 32
    return b // 16, (b // 4) % 4, b % 4, h // 2, h % 2


def send(a, to):
    pairs = [(i, device_of(*to(*place_of(i)))) for i in range(256)]
    return lax.ppermute(a, AXES, pairs)


def along(first, step):
    def to(zl, x, y, zh, c):
        on_x = (c == 0) == first
        return (zl, x + step, y, zh, c) if on_x else (zl, x, y + step, zh, c)

    return to


def key_orders():
    table = np.zeros((256, 32), np.int32)
    for i in range(256):
        zl, x, y, zh, c = place_of(i)
        k = 0
        for s2 in (0, -1, 1, 2):
            for s1 in (0, -1, 1, 2):
                for f in (0, 1):
                    on_x, on_y = (s1, s2) if c == 0 else (s2, s1)
                    table[i, k] = ((zl + f) % 2) * 16 + ((x + on_x) % 4) * 4 + (y + on_y) % 4
                    k += 1
    return table


ORDERS = key_orders()


def exchange_heads(a, zh):
    twice = jnp.concatenate([a, a[:3]], 0)
    mine = lax.dynamic_slice_in_dim(twice, zh, 4, 0)
    got = [mine[0]] + [
        send(mine[s], lambda zl, x, y, z, c, s=s: (zl, x, y, z + s, c)) for s in (1, 2, 3)
    ]
    ring = jnp.stack([got[0], got[3], got[2], got[1], got[0], got[3], got[2]])
    return lax.dynamic_slice_in_dim(ring, (4 - zh) % 4, 4, 0)


def bounds_kernel(pos_ref, seg_ref, out_ref):
    pos, seg = pos_ref[...], seg_ref[...]
    for s in range(1, 4):
        out_ref[s - 1] = jnp.min(jnp.where(seg >= s, pos, NEVER))


def doc_bounds(position, segment):
    return pl.pallas_call(
        bounds_kernel,
        out_shape=jax.ShapeDtypeStruct((8,), jnp.int32),
        out_specs=pl.BlockSpec(memory_space=pltpu.SMEM),
        name="doc_bounds",
    )(position, segment)


def doc_start(meta, at):
    start = jnp.zeros_like(at)
    for s in range(3):
        edge = meta[64 + s]
        start = jnp.maximum(start, jnp.where(edge <= at, edge, 0))
    return start


def flash_kernel(pieces, first_block, carry, final, *refs):
    meta = refs[0]
    q_own, q_oth = refs[1], refs[2]
    piece_refs = refs[3 : 3 + len(pieces)]
    rest = list(refs[3 + len(pieces) :])
    if carry:
        acc_in, ml_in = rest.pop(0), rest.pop(0)
    out_a, out_b = rest.pop(0), rest.pop(0)
    kv, q_s, acc, m_s, l_s, full, part, sems = rest
    core, block = meta[72], meta[73]
    tiles = sum(pieces) // 128

    at = 0
    copies = []
    for i, rows in enumerate(pieces):
        copy = pltpu.make_async_copy(piece_refs[i], kv.at[pl.ds(at, rows), :], sems.at[i])
        copy.start()
        copies.append(copy)
        at += rows

    for hf in range(2):
        for h in range(4):
            rows, cols = pl.ds(hf * 128, 128), pl.ds(h * 128, 128)
            q_s[hf * 4 + h, pl.ds(0, 128), :] = q_own[rows, cols]
            q_s[hf * 4 + h, pl.ds(128, 128), :] = q_oth[rows, cols]
            if carry:
                acc[hf * 4 + h] = acc_in[hf * 4 + h]
                m_s[hf * 4 + h] = jnp.broadcast_to(ml_in[hf, :, h : h + 1], (256, 128))
                lane = lax.broadcasted_iota(jnp.int32, (256, 128), 1)
                l_s[hf * 4 + h] = jnp.where(lane == 0, ml_in[hf, :, 4 + h : 5 + h], 0.0)
            else:
                acc[hf * 4 + h] = jnp.zeros((256, 128), jnp.float32)
                m_s[hf * 4 + h] = jnp.full((256, 128), MASKED, jnp.float32)
                l_s[hf * 4 + h] = jnp.zeros((256, 128), jnp.float32)

    for copy in copies:
        copy.wait()

    row = lax.broadcasted_iota(jnp.int32, (256, 128), 0)
    lane = lax.broadcasted_iota(jnp.int32, (256, 128), 1)
    own_row = row < 128
    in_half = jnp.where(own_row, row, row - 128)
    q_core = jnp.where(own_row, core, 1 - core)
    q_off = jnp.where(in_half >= 64, in_half + 64, in_half) + q_core * 64
    k_off = jnp.where(lane >= 64, lane + 64, lane) + core * 64

    def base_of(tile):
        source = meta[80 + first_block + tile // 2]
        return meta[source * 2 + tile % 2]

    def step(hf, tile_a, tile_b, masks):
        k_a = kv[pl.ds(pl.multiple_of(tile_a * 128, 128), 128), :]
        k_b = kv[pl.ds(pl.multiple_of(tile_b * 128, 128), 128), :]
        k = jnp.concatenate([k_a[:, :D], k_b[:, :D]], 0)
        v = jnp.concatenate([k_a[:, D:], k_b[:, D:]], 0)
        for h in range(4):
            i = hf * 4 + h
            s = lax.dot_general(
                q_s[i], k, (((1,), (1,)), ((), ())), preferred_element_type=jnp.float32
            )
            s_a, s_b = s[:, :128], s[:, 128:]
            if masks is not None:
                s_a = jnp.where(masks[0], s_a, MASKED)
                s_b = jnp.where(masks[1], s_b, MASKED)
            top = jnp.max(jnp.maximum(s_a, s_b), axis=1, keepdims=True)
            old = m_s[i]
            new = jnp.maximum(old, top)
            p_a = jnp.exp2((s_a - new) * LOG2E_SCALE)
            p_b = jnp.exp2((s_b - new) * LOG2E_SCALE)
            fade = jnp.exp2((old - new) * LOG2E_SCALE)
            l_s[i] = l_s[i] * fade + (p_a + p_b)
            m_s[i] = new
            p = jnp.concatenate([p_a.astype(jnp.bfloat16), p_b.astype(jnp.bfloat16)], 1)
            acc[i] = acc[i] * fade + jnp.dot(p, v, preferred_element_type=jnp.float32)

    for hf in range(2):
        qb = meta[block * 2 + hf]
        lo_first, lo_last = doc_start(meta, qb), doc_start(meta, qb + 255)

        def classify(tile, counts):
            n_full, n_part = counts
            kb = base_of(tile)
            seen = (kb <= qb) & (kb + 255 >= lo_first)
            whole = (kb < qb) & (kb >= lo_last)
            full[n_full] = tile
            part[n_part] = tile
            return (
                n_full + jnp.where(seen & whole, 1, 0),
                n_part + jnp.where(seen & jnp.logical_not(whole), 1, 0),
            )

        n_full, n_part = lax.fori_loop(0, tiles, classify, (jnp.int32(0), jnp.int32(0)))
        odd = n_full % 2
        last = full[jnp.maximum(n_full - 1, 0)]
        part[n_part] = jnp.where(odd == 1, last, part[n_part])
        n_part = n_part + odd

        def whole_pair(j, _):
            step(hf, full[2 * j], full[2 * j + 1], None)
            return 0

        lax.fori_loop(0, n_full // 2, whole_pair, 0)

        q_pos = qb + q_off
        q_lo = doc_start(meta, q_pos)

        def part_pair(j, _):
            tile_a = part[2 * j]
            there = 2 * j + 1 < n_part
            tile_b = jnp.where(there, part[2 * j + 1], tile_a)
            k_a = base_of(tile_a) + k_off
            k_b = jnp.where(there, base_of(tile_b), NEVER) + k_off
            masks = ((k_a <= q_pos) & (k_a >= q_lo), (k_b <= q_pos) & (k_b >= q_lo))
            step(hf, tile_a, tile_b, masks)
            return 0

        lax.fori_loop(0, (n_part + 1) // 2, part_pair, 0)

        stats = jnp.zeros((256, 128), jnp.float32)
        for h in range(4):
            total = jnp.sum(l_s[hf * 4 + h], axis=1, keepdims=True)
            stats = jnp.where(lane == h, m_s[hf * 4 + h], stats)
            stats = jnp.where(lane == 4 + h, total, stats)
            if final:
                a = acc[hf * 4 + h]
                out_a[pl.ds(hf * 128, 128), pl.ds(h * 128, 128)] = a[:128]
                out_b[pl.ds(hf * 128, 128), pl.ds(h * 128, 128)] = a[128:]
            else:
                out_a[hf * 4 + h] = acc[hf * 4 + h]
        if final:
            out_a[pl.ds(hf * 128, 128), pl.ds(512, 128)] = stats[:128]
            out_b[pl.ds(hf * 128, 128), pl.ds(512, 128)] = stats[128:]
        else:
            out_b[hf] = stats


def flash(meta, q_own, q_oth, pieces, first_block, state, final):
    rows = tuple(p.shape[0] for p in pieces)
    carry = state is not None
    keys = sum(rows)
    if final:
        shapes = [jax.ShapeDtypeStruct((256, 640), jnp.float32)] * 2
    else:
        shapes = [
            jax.ShapeDtypeStruct((8, 256, 128), jnp.float32),
            jax.ShapeDtypeStruct((2, 256, 128), jnp.float32),
        ]
    vmem = pl.BlockSpec(memory_space=pltpu.VMEM)
    in_specs = [pl.BlockSpec(memory_space=pltpu.SMEM), vmem, vmem]
    in_specs += [pl.BlockSpec(memory_space=pl.ANY)] * len(pieces)
    in_specs += [vmem] * (2 if carry else 0)
    return pl.pallas_call(
        functools.partial(flash_kernel, rows, first_block, carry, final),
        out_shape=shapes,
        in_specs=in_specs,
        out_specs=[vmem, vmem],
        scratch_shapes=[
            pltpu.VMEM((keys, 256), jnp.bfloat16),
            pltpu.VMEM((8, 256, 128), jnp.bfloat16),
            pltpu.VMEM((8, 256, 128), jnp.float32),
            pltpu.VMEM((8, 256, 128), jnp.float32),
            pltpu.VMEM((8, 256, 128), jnp.float32),
            pltpu.SMEM((keys // 128 + 2,), jnp.int32),
            pltpu.SMEM((keys // 128 + 2,), jnp.int32),
            pltpu.SemaphoreType.DMA((len(pieces),)),
        ],
        compiler_params=pltpu.CompilerParams(vmem_limit_bytes=VMEM_LIMIT),
        cost_estimate=pl.CostEstimate(
            flops=2048 * keys * D * 2, bytes_accessed=keys * 512, transcendentals=1024 * keys
        ),
        name="flash",
    )(meta, q_own, q_oth, *pieces, *(state if carry else ()))


def merge_kernel(a_ref, b_ref, out_ref):
    sa, sb = a_ref[:, 512:640], b_ref[:, 512:640]
    top = jnp.maximum(sa, sb)
    wa = jnp.exp2((sa - top) * LOG2E_SCALE)
    wb = jnp.exp2((sb - top) * LOG2E_SCALE)
    for h in range(4):
        fa, fb = wa[:, h : h + 1], wb[:, h : h + 1]
        total = sa[:, 4 + h : 5 + h] * fa + sb[:, 4 + h : 5 + h] * fb
        cols = pl.ds(h * 128, 128)
        mixed = a_ref[:, cols] * fa + b_ref[:, cols] * fb
        out_ref[:, cols] = (mixed / total).astype(jnp.bfloat16)


def merge(a, b):
    return pl.pallas_call(
        merge_kernel, out_shape=jax.ShapeDtypeStruct((256, 512), jnp.bfloat16), name="merge"
    )(a, b)


def other_core(zl, x, y, zh, c):
    return (zl, x, y, zh, c + 1)


def other_lo(zl, x, y, zh, c):
    return (zl + 1, x, y, zh, c)


def local(queries, keys, values, position, segment):
    head, blk = lax.axis_index("head"), lax.axis_index("blk")
    zh, core = head // 2, head % 2
    bases = position.reshape(32, 2, 256)[:, :, 0].reshape(64)
    order = lax.dynamic_slice(jnp.asarray(ORDERS), (head * 32 + blk, 0), (1, 32)).reshape(32)
    ids = jnp.stack([core, blk] + [jnp.int32(0)] * 6).astype(jnp.int32)
    meta = jnp.concatenate([bases, doc_bounds(position, segment), ids, order])

    with jax.named_scope("kv_heads"):
        kv = jnp.concatenate([keys.reshape(64, KV, D), values.reshape(64, KV, D)], 2)
        kv = exchange_heads(kv.transpose(1, 0, 2), zh).reshape(256, 256)
    with jax.named_scope("kv_z"):
        own = jnp.concatenate([kv, send(kv, other_lo)], 0)
    with jax.named_scope("kv_first"):
        line = [own, send(own, along(True, 1)), send(own, along(True, -1)), send(own, along(True, 2))]
        line = jnp.concatenate(line, 0)
    with jax.named_scope("kv_second"):
        up, down = send(line, along(False, 1)), send(line, along(False, -1))
        half_a, half_b = send(up[:1024], along(False, 1)), send(down[1024:], along(False, -1))
    with jax.named_scope("q_heads"):
        q_own = exchange_heads(queries.reshape(64, 4, 512).transpose(1, 0, 2), zh).reshape(256, 512)
        q_oth = send(q_own, other_core)
    with jax.named_scope("attend"):
        state = flash(meta, q_own, q_oth, [line], 0, None, False)
        state = flash(meta, q_own, q_oth, [up, down], 8, state, False)
        mine, theirs = flash(meta, q_own, q_oth, [half_a, half_b], 24, state, True)
    with jax.named_scope("merge"):
        out = merge(mine, send(theirs, other_core))
    with jax.named_scope("out_heads"):
        out = exchange_heads(out.reshape(4, 64, 512), zh)
    return out.transpose(1, 0, 2).reshape(1, 64, HEADS * D)


def solution(mesh):
    spec = P("blk", "head", None)
    return jax.shard_map(
        local,
        mesh=mesh,
        in_specs=(spec, spec, spec, P(), P()),
        out_specs=spec,
        check_vma=False,
    )
```

```python
import functools

import jax
import jax.numpy as jnp
import numpy as np
from jax import lax
from jax.experimental import pallas as pl
from jax.experimental.pallas import tpu as pltpu
from jax.sharding import PartitionSpec as P

HEADS = 16
KV = 4
D = 128
AXES = ("head", "blk")
NEVER = 1 << 20
MASKED = -1e30
LOG2E_SCALE = float(np.log2(np.e) * D**-0.5)
VMEM_LIMIT = 40 * 1024 * 1024
SMALL_LIMIT = 8 * 1024 * 1024


def device_of(zl, x, y, zh, c):
    return ((zh % 4) * 2 + c % 2) * 32 + (zl % 2) * 16 + (x % 4) * 4 + y % 4


def place_of(device):
    h, b = device // 32, device % 32
    return b // 16, (b // 4) % 4, b % 4, h // 2, h % 2


def send(a, to):
    pairs = [(i, device_of(*to(*place_of(i)))) for i in range(256)]
    return lax.ppermute(a, AXES, pairs)


def along(first, step):
    def to(zl, x, y, zh, c):
        on_x = (c == 0) == first
        return (zl, x + step, y, zh, c) if on_x else (zl, x, y + step, zh, c)

    return to


def key_orders():
    table = np.zeros((256, 32), np.int32)
    for i in range(256):
        zl, x, y, zh, c = place_of(i)
        k = 0
        for s2 in (0, -1, 1, 2):
            for s1 in (0, -1, 1, 2):
                for f in (0, 1):
                    on_x, on_y = (s1, s2) if c == 0 else (s2, s1)
                    table[i, k] = ((zl + f) % 2) * 16 + ((x + on_x) % 4) * 4 + (y + on_y) % 4
                    k += 1
    return table


ORDERS = key_orders()


def pack_kernel(zh_ref, *refs):
    ins, outs = refs[:-4], refs[-4:]
    for s, out in enumerate(outs):
        head = lax.rem(zh_ref[0] + s, 4)
        at = 0
        for a in ins:
            width = a.shape[1] // 4
            cols = pl.ds(pl.multiple_of(head * width, width), width)
            out[:, pl.ds(at, width)] = a[:, cols]
            at += width


def pack(zh, *arrays):
    width = sum(a.shape[1] for a in arrays) // 4
    vmem = pl.BlockSpec(memory_space=pltpu.VMEM)
    return pl.pallas_call(
        pack_kernel,
        out_shape=[jax.ShapeDtypeStruct((64, width), jnp.bfloat16)] * 4,
        in_specs=[pl.BlockSpec(memory_space=pltpu.SMEM)] + [vmem] * len(arrays),
        out_specs=[vmem] * 4,
        compiler_params=pltpu.CompilerParams(vmem_limit_bytes=SMALL_LIMIT),
        name="pack",
    )(zh, *arrays)


def unpack_kernel(by_rows, zh_ref, *refs):
    out = refs[-1]
    for s in range(4):
        z = lax.rem(zh_ref[0] + 4 - s, 4)
        a = refs[s]
        if by_rows:
            out[pl.ds(pl.multiple_of(z * 64, 64), 64), :] = a[...]
        else:
            out[:, pl.ds(pl.multiple_of(z * 512, 512), 512)] = a[...]


def unpack(zh, arrays, by_rows):
    width = arrays[0].shape[1]
    shape = (256, width) if by_rows else (64, 4 * width)
    vmem = pl.BlockSpec(memory_space=pltpu.VMEM)
    return pl.pallas_call(
        functools.partial(unpack_kernel, by_rows),
        out_shape=jax.ShapeDtypeStruct(shape, jnp.bfloat16),
        in_specs=[pl.BlockSpec(memory_space=pltpu.SMEM)] + [vmem] * 4,
        out_specs=vmem,
        compiler_params=pltpu.CompilerParams(vmem_limit_bytes=SMALL_LIMIT),
        name="unpack",
    )(zh, *arrays)


def over_z(arrays):
    return [arrays[0]] + [
        send(arrays[s], lambda zl, x, y, z, c, s=s: (zl, x, y, z + s, c)) for s in (1, 2, 3)
    ]


PLAN = 72
Q_AT = 6 * PLAN
CHUNKS = ((0, 8), (8, 16), (24, 8))


def doc_start(meta, at):
    start = jnp.zeros_like(at)
    for s in range(3):
        edge = meta[Q_AT + 3 + s]
        start = jnp.maximum(start, jnp.where(edge <= at, edge, 0))
    return start


def plan_kernel(pos_ref, seg_ref, base_ref, order_ref, ids_ref, plan):
    pos, seg = pos_ref[...], seg_ref[...]
    for s in range(1, 4):
        plan[Q_AT + 2 + s] = jnp.min(jnp.where(seg >= s, pos, NEVER))
    plan[Q_AT + 2] = ids_ref[0]
    for hf in range(2):
        qb = base_ref[ids_ref[1] * 2 + hf]
        plan[Q_AT + hf] = qb
        lo_first, lo_last = doc_start(plan, qb), doc_start(plan, qb + 255)
        for chunk, (first, blocks) in enumerate(CHUNKS):
            off = (chunk * 2 + hf) * PLAN

            def classify(i, counts):
                n_full, n_part = counts
                source = order_ref[first + i]
                for t in range(2):
                    kb = base_ref[source * 2 + t]
                    seen = (kb <= qb) & (kb + 255 >= lo_first)
                    whole = seen & (kb < qb) & (kb >= lo_last)
                    entry = (i * 2 + t) + kb * 256
                    plan[off + 2 + n_full] = entry
                    plan[off + 36 + n_part] = entry
                    n_full = n_full + jnp.where(whole, 1, 0)
                    n_part = n_part + jnp.where(seen & jnp.logical_not(whole), 1, 0)
                return n_full, n_part

            n_full, n_part = lax.fori_loop(0, blocks, classify, (jnp.int32(0), jnp.int32(0)))
            odd = n_full % 2
            last = plan[off + 2 + jnp.maximum(n_full - 1, 0)]
            plan[off + 36 + n_part] = jnp.where(odd == 1, last, plan[off + 36 + n_part])
            plan[off] = n_full
            plan[off + 1] = n_part + odd


def make_plan(position, segment, bases, order, ids):
    smem, vmem = (pl.BlockSpec(memory_space=m) for m in (pltpu.SMEM, pltpu.VMEM))
    return pl.pallas_call(
        plan_kernel,
        out_shape=jax.ShapeDtypeStruct((Q_AT + 8,), jnp.int32),
        in_specs=[vmem, vmem, smem, smem, smem],
        out_specs=smem,
        compiler_params=pltpu.CompilerParams(vmem_limit_bytes=SMALL_LIMIT),
        name="plan",
    )(position, segment, bases, order, ids)


def flash_kernel(pieces, chunk, carry, final, *refs):
    meta = refs[0]
    q_own, q_oth = refs[1], refs[2]
    piece_refs = refs[3 : 3 + len(pieces)]
    rest = list(refs[3 + len(pieces) :])
    if carry:
        acc_in, ml_in = rest.pop(0), rest.pop(0)
    out_a, out_b = rest.pop(0), rest.pop(0)
    kv, kt, q_s, acc, m_s, l_s, sems = rest
    core = meta[Q_AT + 2]
    tiles = sum(pieces) // 128

    at = 0
    copies = []
    for i, rows in enumerate(pieces):
        copy = pltpu.make_async_copy(piece_refs[i], kv.at[pl.ds(at, rows), :], sems.at[i])
        copy.start()
        copies.append(copy)
        at += rows

    for hf in range(2):
        for h in range(4):
            rows, cols = pl.ds(hf * 128, 128), pl.ds(h * 128, 128)
            q_s[hf * 4 + h, pl.ds(0, 128), :] = q_own[rows, cols]
            q_s[hf * 4 + h, pl.ds(128, 128), :] = q_oth[rows, cols]
            if carry:
                acc[hf * 4 + h] = acc_in[hf * 4 + h]
                m_s[hf * 4 + h] = jnp.broadcast_to(ml_in[hf, :, h : h + 1], (256, 128))
                lane = lax.broadcasted_iota(jnp.int32, (256, 128), 1)
                l_s[hf * 4 + h] = jnp.where(lane == 0, ml_in[hf, :, 4 + h : 5 + h], 0.0)
            else:
                acc[hf * 4 + h] = jnp.zeros((256, 128), jnp.float32)
                m_s[hf * 4 + h] = jnp.full((256, 128), MASKED, jnp.float32)
                l_s[hf * 4 + h] = jnp.zeros((256, 128), jnp.float32)

    for copy in copies:
        copy.wait()
    for t in range(tiles):
        kt[t] = kv[pl.ds(t * 128, 128), pl.ds(0, D)].T

    row = lax.broadcasted_iota(jnp.int32, (256, 128), 0)
    lane = lax.broadcasted_iota(jnp.int32, (256, 128), 1)
    own_row = row < 128
    in_half = jnp.where(own_row, row, row - 128)
    q_core = jnp.where(own_row, core, 1 - core)
    q_off = jnp.where(in_half >= 64, in_half + 64, in_half) + q_core * 64
    k_off = jnp.where(lane >= 64, lane + 64, lane) + core * 64

    def step(hf, tile_a, tile_b, masks):
        k_a = kv[pl.ds(pl.multiple_of(tile_a * 128, 128), 128), :]
        k_b = kv[pl.ds(pl.multiple_of(tile_b * 128, 128), 128), :]
        k = jnp.concatenate([kt[tile_a], kt[tile_b]], 1)
        v = jnp.concatenate([k_a[:, D:], k_b[:, D:]], 0)
        ss = [
            lax.dot_general(
                q_s[hf * 4 + h], k, (((1,), (0,)), ((), ())), preferred_element_type=jnp.float32
            )
            for h in range(4)
        ]
        ps, fades = [], []
        for h in range(4):
            i = hf * 4 + h
            s_a, s_b = ss[h][:, :128], ss[h][:, 128:]
            if masks is not None:
                s_a = jnp.where(masks[0], s_a, MASKED)
                s_b = jnp.where(masks[1], s_b, MASKED)
            old = m_s[i]
            new = jnp.maximum(old, jnp.max(jnp.maximum(s_a, s_b), axis=1, keepdims=True))
            m_s[i] = new
            p_a = jnp.exp2((s_a - new) * LOG2E_SCALE)
            p_b = jnp.exp2((s_b - new) * LOG2E_SCALE)
            fades.append(jnp.exp2((old - new) * LOG2E_SCALE))
            l_s[i] = l_s[i] * fades[-1] + p_a + p_b
            ps.append(jnp.concatenate([p_a.astype(jnp.bfloat16), p_b.astype(jnp.bfloat16)], 1))
        for h in range(4):
            i = hf * 4 + h
            acc[i] = acc[i] * fades[h] + jnp.dot(ps[h], v, preferred_element_type=jnp.float32)

    def quad(hf, tiles4):
        kk = [kv[pl.ds(pl.multiple_of(t * 128, 128), 128), :] for t in tiles4]
        k = jnp.concatenate([kt[t] for t in tiles4], 1)
        v = jnp.concatenate([a[:, D:] for a in kk], 0)
        ss = [
            lax.dot_general(
                q_s[hf * 4 + h], k, (((1,), (0,)), ((), ())), preferred_element_type=jnp.float32
            )
            for h in range(4)
        ]
        ps, fades = [], []
        for h in range(4):
            i = hf * 4 + h
            st = [ss[h][:, t * 128 : t * 128 + 128] for t in range(4)]
            top = jnp.maximum(jnp.maximum(st[0], st[1]), jnp.maximum(st[2], st[3]))
            old = m_s[i]
            new = jnp.maximum(old, jnp.max(top, axis=1, keepdims=True))
            m_s[i] = new
            p = [jnp.exp2((a - new) * LOG2E_SCALE) for a in st]
            fades.append(jnp.exp2((old - new) * LOG2E_SCALE))
            l_s[i] = l_s[i] * fades[-1] + (p[0] + p[1]) + (p[2] + p[3])
            ps.append(jnp.concatenate([a.astype(jnp.bfloat16) for a in p], 1))
        for h in range(4):
            i = hf * 4 + h
            acc[i] = acc[i] * fades[h] + jnp.dot(ps[h], v, preferred_element_type=jnp.float32)

    for hf in range(2):
        qb = meta[Q_AT + hf]
        off = (chunk * 2 + hf) * PLAN
        n_full, n_part = meta[off], meta[off + 1]

        def whole(j):
            return meta[off + 2 + j] & 255

        def whole_quad(j, _):
            quad(hf, [whole(4 * j + t) for t in range(4)])
            return 0

        lax.fori_loop(0, n_full // 4, whole_quad, 0)

        def whole_pair(j, _):
            step(hf, whole(2 * j), whole(2 * j + 1), None)
            return 0

        lax.fori_loop(n_full // 4 * 2, n_full // 2, whole_pair, 0)

        q_pos = qb + q_off
        q_lo = doc_start(meta, q_pos)

        def part_pair(j, _):
            there = 2 * j + 1 < n_part
            e_a = meta[off + 36 + 2 * j]
            e_b = jnp.where(there, meta[off + 37 + 2 * j], e_a)
            tile_a, tile_b = e_a & 255, e_b & 255
            k_a = (e_a >> 8) + k_off
            k_b = jnp.where(there, e_b >> 8, NEVER) + k_off
            masks = ((k_a <= q_pos) & (k_a >= q_lo), (k_b <= q_pos) & (k_b >= q_lo))
            step(hf, tile_a, tile_b, masks)
            return 0

        lax.fori_loop(0, (n_part + 1) // 2, part_pair, 0)

        stats = jnp.zeros((256, 128), jnp.float32)
        for h in range(4):
            total = jnp.sum(l_s[hf * 4 + h], axis=1, keepdims=True)
            stats = jnp.where(lane == h, m_s[hf * 4 + h], stats)
            stats = jnp.where(lane == 4 + h, total, stats)
            if final:
                a = acc[hf * 4 + h]
                out_a[pl.ds(hf * 128, 128), pl.ds(h * 128, 128)] = a[:128]
                out_b[pl.ds(hf * 128, 128), pl.ds(h * 128, 128)] = a[128:]
            else:
                out_a[hf * 4 + h] = acc[hf * 4 + h]
        if final:
            out_a[pl.ds(hf * 128, 128), pl.ds(512, 128)] = stats[:128]
            out_b[pl.ds(hf * 128, 128), pl.ds(512, 128)] = stats[128:]
        else:
            out_b[hf] = stats


def flash(meta, q_own, q_oth, pieces, chunk, state, final):
    rows = tuple(p.shape[0] for p in pieces)
    carry = state is not None
    keys = sum(rows)
    if final:
        shapes = [jax.ShapeDtypeStruct((256, 640), jnp.float32)] * 2
    else:
        shapes = [
            jax.ShapeDtypeStruct((8, 256, 128), jnp.float32),
            jax.ShapeDtypeStruct((2, 256, 128), jnp.float32),
        ]
    vmem = pl.BlockSpec(memory_space=pltpu.VMEM)
    in_specs = [pl.BlockSpec(memory_space=pltpu.SMEM), vmem, vmem]
    in_specs += [pl.BlockSpec(memory_space=pl.ANY)] * len(pieces)
    in_specs += [vmem] * (2 if carry else 0)
    return pl.pallas_call(
        functools.partial(flash_kernel, rows, chunk, carry, final),
        out_shape=shapes,
        in_specs=in_specs,
        out_specs=[vmem, vmem],
        scratch_shapes=[
            pltpu.VMEM((keys, 256), jnp.bfloat16),
            pltpu.VMEM((keys // 128, 128, 128), jnp.bfloat16),
            pltpu.VMEM((8, 256, 128), jnp.bfloat16),
            pltpu.VMEM((8, 256, 128), jnp.float32),
            pltpu.VMEM((8, 256, 128), jnp.float32),
            pltpu.VMEM((8, 256, 128), jnp.float32),
            pltpu.SemaphoreType.DMA((len(pieces),)),
        ],
        compiler_params=pltpu.CompilerParams(vmem_limit_bytes=VMEM_LIMIT),
        cost_estimate=pl.CostEstimate(
            flops=2048 * keys * D * 24, bytes_accessed=keys * 512, transcendentals=1024 * keys
        ),
        name="flash",
    )(meta, q_own, q_oth, *pieces, *(state if carry else ()))


def merge_kernel(zh_ref, a_ref, b_ref, *outs):
    for s, out in enumerate(outs):
        z = lax.rem(zh_ref[0] + s, 4)
        rows = pl.ds(pl.multiple_of(z * 64, 64), 64)
        sa, sb = a_ref[rows, pl.ds(512, 128)], b_ref[rows, pl.ds(512, 128)]
        top = jnp.maximum(sa, sb)
        wa = jnp.exp2((sa - top) * LOG2E_SCALE)
        wb = jnp.exp2((sb - top) * LOG2E_SCALE)
        total = sa[:, 4:8] * wa[:, 0:4] + sb[:, 4:8] * wb[:, 0:4]
        wa, wb = wa[:, 0:4] / total, wb[:, 0:4] / total
        for h in range(4):
            cols = pl.ds(h * 128, 128)
            mixed = a_ref[rows, cols] * wa[:, h : h + 1] + b_ref[rows, cols] * wb[:, h : h + 1]
            out[:, cols] = mixed.astype(jnp.bfloat16)


def merge(zh, a, b):
    vmem = pl.BlockSpec(memory_space=pltpu.VMEM)
    return pl.pallas_call(
        merge_kernel,
        out_shape=[jax.ShapeDtypeStruct((64, 512), jnp.bfloat16)] * 4,
        in_specs=[pl.BlockSpec(memory_space=pltpu.SMEM), vmem, vmem],
        out_specs=[vmem] * 4,
        compiler_params=pltpu.CompilerParams(vmem_limit_bytes=SMALL_LIMIT),
        name="merge",
    )(zh, a, b)


def other_core(zl, x, y, zh, c):
    return (zl, x, y, zh, c + 1)


def other_lo(zl, x, y, zh, c):
    return (zl + 1, x, y, zh, c)


def after(first, *then):
    return lax.optimization_barrier((first, *then))[1:]


def local(queries, keys, values, position, segment):
    head, blk = lax.axis_index("head"), lax.axis_index("blk")
    zh, core = head // 2, head % 2
    zh = zh.astype(jnp.int32).reshape(1)

    with jax.named_scope("kv_heads"):
        kv = unpack(zh, over_z(pack(zh, keys.reshape(64, 512), values.reshape(64, 512))), True)
    with jax.named_scope("kv_z"):
        own = jnp.concatenate([kv, send(kv, other_lo)], 0)
    with jax.named_scope("kv_first"):
        line = [own, send(own, along(True, 1)), send(own, along(True, -1)), send(own, along(True, 2))]
        line = jnp.concatenate(line, 0)
    with jax.named_scope("q_heads"):
        queries, position, segment = after(own, queries, position, segment)
        q_own = unpack(zh, over_z(pack(zh, queries.reshape(64, 2048))), True)
        q_oth = send(q_own, other_core)
    with jax.named_scope("plan"):
        position, segment = after(line, position, segment)
        bases = position.reshape(32, 2, 256)[:, :, 0].reshape(64)
        order = lax.dynamic_slice(jnp.asarray(ORDERS), (head * 32 + blk, 0), (1, 32)).reshape(32)
        ids = jnp.stack([core, blk]).astype(jnp.int32)
        plan = make_plan(position, segment, bases, order, ids)
    with jax.named_scope("kv_second"):
        up, down = send(line, along(False, 1)), send(line, along(False, -1))
        half_a, half_b = send(up[:1024], along(False, 1)), send(down[1024:], along(False, -1))
    with jax.named_scope("attend"):
        state = flash(plan, q_own, q_oth, [line], 0, None, False)
        state = flash(plan, q_own, q_oth, [up, down], 1, state, False)
        mine, theirs = flash(plan, q_own, q_oth, [half_a, half_b], 2, state, True)
    with jax.named_scope("merge"):
        parts = merge(zh, mine, send(theirs, other_core))
    with jax.named_scope("out_heads"):
        out = unpack(zh, over_z(parts), False)
    return out.reshape(1, 64, HEADS * D)


def solution(mesh):
    spec = P("blk", "head", None)
    return jax.shard_map(
        local,
        mesh=mesh,
        in_specs=(spec, spec, spec, P(), P()),
        out_specs=spec,
        check_vma=False,
    )
```

```python
import functools

import jax
import jax.numpy as jnp
import numpy as np
from jax import lax
from jax.experimental import pallas as pl
from jax.experimental.pallas import tpu as pltpu
from jax.sharding import PartitionSpec as P

HEADS = 16
KV = 4
D = 128
AXES = ("head", "blk")
NEVER = 1 << 20
MASKED = -1e30
LOG2E_SCALE = float(np.log2(np.e) * D**-0.5)
VMEM_LIMIT = 32 * 1024 * 1024
SMALL_LIMIT = 8 * 1024 * 1024


def device_of(zl, x, y, zh, c):
    return ((zh % 4) * 2 + c % 2) * 32 + (zl % 2) * 16 + (x % 4) * 4 + y % 4


def place_of(device):
    h, b = device // 32, device % 32
    return b // 16, (b // 4) % 4, b % 4, h // 2, h % 2


def send(a, to):
    pairs = [(i, device_of(*to(*place_of(i)))) for i in range(256)]
    return lax.ppermute(a, AXES, pairs)


def along(first, step):
    def to(zl, x, y, zh, c):
        on_x = (c == 0) == first
        return (zl, x + step, y, zh, c) if on_x else (zl, x, y + step, zh, c)

    return to


SHIFTS = (0, 3, 1, 2)


def my_z():
    return lax.axis_index("head") // 2


def pack_kernel(*refs):
    ins, outs, sems = refs[:-5], refs[-5:-1], refs[-1]
    copies = []
    for s, out in enumerate(outs):
        head = lax.rem(my_z() + s, 4)
        at = 0
        for i, a in enumerate(ins):
            width = a.shape[1] // 4
            cols = pl.ds(pl.multiple_of(head * width, width), width)
            copy = pltpu.make_async_copy(a.at[:, cols], out.at[:, pl.ds(at, width)], sems.at[s, i])
            copy.start()
            copies.append(copy)
            at += width
    for copy in copies:
        copy.wait()


def pack(*arrays):
    width = sum(a.shape[1] for a in arrays) // 4
    vmem = pl.BlockSpec(memory_space=pltpu.VMEM)
    return pl.pallas_call(
        pack_kernel,
        out_shape=[jax.ShapeDtypeStruct((64, width), jnp.bfloat16)] * 4,
        in_specs=[pl.BlockSpec(memory_space=pl.ANY)] * len(arrays),
        out_specs=[vmem] * 4,
        scratch_shapes=[pltpu.SemaphoreType.DMA((4, len(arrays)))],
        name="pack",
    )(*arrays)


def unpack_kernel(*refs):
    outs = refs[4:]
    for s in range(4):
        z = lax.rem(my_z() + 4 - s, 4)
        at = 0
        for out in outs:
            width = out.shape[1]
            out[pl.ds(pl.multiple_of(z * 64, 64), 64), :] = refs[s][:, pl.ds(at, width)]
            at += width


def unpack(arrays, widths):
    vmem = pl.BlockSpec(memory_space=pltpu.VMEM)
    return pl.pallas_call(
        unpack_kernel,
        out_shape=[jax.ShapeDtypeStruct((256, w), jnp.bfloat16) for w in widths],
        in_specs=[vmem] * 4,
        out_specs=[vmem] * len(widths),
        compiler_params=pltpu.CompilerParams(vmem_limit_bytes=SMALL_LIMIT),
        name="unpack",
    )(*arrays)


def finish_kernel(*refs):
    for s in range(4):
        z = lax.rem(my_z() + 4 - s, 4)
        refs[4][:, pl.ds(pl.multiple_of(z * 512, 512), 512)] = refs[s][...]


def finish(arrays):
    vmem = pl.BlockSpec(memory_space=pltpu.VMEM)
    return pl.pallas_call(
        finish_kernel,
        out_shape=jax.ShapeDtypeStruct((64, HEADS * D), jnp.bfloat16),
        in_specs=[vmem] * 4,
        out_specs=vmem,
        compiler_params=pltpu.CompilerParams(vmem_limit_bytes=SMALL_LIMIT),
        name="finish",
    )(*arrays)


def over_z(arrays):
    return [arrays[0]] + [
        send(arrays[s], lambda zl, x, y, z, c, s=s: (zl, x, y, z + s, c)) for s in (1, 2, 3)
    ]


CALLS = ((1, 0, 16, 1), (0, 0, 16, 24))
PLAN = 72
Q_AT = 2 * len(CALLS) * PLAN
CORE_AT = Q_AT + 4
EDGE_AT = Q_AT + 5


def doc_start(meta, at):
    start = jnp.zeros_like(at)
    for s in range(3):
        edge = meta[EDGE_AT + s]
        start = jnp.maximum(start, jnp.where(edge <= at, edge, 0))
    return start


def plan_kernel(pos_hbm, seg_hbm, behind, plan, first_ref, pos_ref, seg_ref, sems):
    core, block = lax.rem(lax.axis_index("head"), 2), lax.axis_index("blk")
    runs = [
        pltpu.make_async_copy(pos_hbm.at[:, pl.ds(h * 256, 128)], first_ref.at[h], sems.at[h])
        for h in range(2)
    ]
    whole = [
        pltpu.make_async_copy(pos_hbm, pos_ref, sems.at[2]),
        pltpu.make_async_copy(seg_hbm, seg_ref, sems.at[3]),
    ]
    for copy in whole + runs:
        copy.start()
    for copy in whole:
        copy.wait()
    zl, x, y = block // 16, (block // 4) % 4, block % 4
    pos, seg = pos_ref[...], seg_ref[...]
    for s in range(1, 4):
        plan[EDGE_AT + s - 1] = jnp.min(jnp.where(seg >= s, pos, NEVER))
    plan[CORE_AT] = core
    for copy in runs:
        copy.wait()
    queries = []
    for whose in range(2):
        for hf in range(2):
            qb = first_ref[hf, (block + 16 * whose) % 32, 0]
            plan[Q_AT + whose * 2 + hf] = qb
            queries.append((qb, doc_start(plan, qb), doc_start(plan, qb + 255)))
    for call, (whose, first, blocks, _) in enumerate(CALLS):
        counts = [[jnp.int32(0), jnp.int32(0)] for _ in range(2)]
        for k in range(first, first + blocks):
            s1, s2 = SHIFTS[k % 4], SHIFTS[k // 4]
            on_x, on_y = jnp.where(core == 0, s1, s2), jnp.where(core == 0, s2, s1)
            source = zl * 16 + (x + on_x) % 4 * 4 + (y + on_y) % 4
            for t in range(2):
                kb = first_ref[t, source, 0]
                entry = ((k - first) * 2 + t) + kb * 256
                for hf in range(2):
                    off = (call * 2 + hf) * PLAN
                    qb, lo_first, lo_last = queries[whose * 2 + hf]
                    n_full, n_part = counts[hf]
                    seen = (kb <= qb) & (kb + 255 >= lo_first)
                    whole = seen & (kb < qb) & (kb >= lo_last)
                    plan[off + 2 + n_full] = entry
                    plan[off + 36 + n_part] = entry
                    counts[hf][0] = n_full + jnp.where(whole, 1, 0)
                    counts[hf][1] = n_part + jnp.where(seen & jnp.logical_not(whole), 1, 0)
        for hf in range(2):
            off = (call * 2 + hf) * PLAN
            n_full, n_part = counts[hf]
            odd = n_full % 2
            last = plan[off + 2 + jnp.maximum(n_full - 1, 0)]
            plan[off + 36 + n_part] = jnp.where(odd == 1, last, plan[off + 36 + n_part])
            plan[off] = n_full
            plan[off + 1] = n_part + odd


def make_plan(position, segment, behind):
    return pl.pallas_call(
        plan_kernel,
        out_shape=jax.ShapeDtypeStruct((EDGE_AT + 3,), jnp.int32),
        in_specs=[pl.BlockSpec(memory_space=pl.ANY)] * 3,
        out_specs=pl.BlockSpec(memory_space=pltpu.SMEM),
        scratch_shapes=[
            pltpu.SMEM((2, 32, 128), jnp.int32),
            pltpu.VMEM((32, 512), jnp.int32),
            pltpu.VMEM((32, 512), jnp.int32),
            pltpu.SemaphoreType.DMA((4,)),
        ],
        name="plan",
    )(position, segment, behind)


def three_parts(log_sum):
    lane = lax.broadcasted_iota(jnp.int32, log_sum.shape, 1)
    high = log_sum.astype(jnp.bfloat16).astype(jnp.float32)
    rest = log_sum - high
    mid = rest.astype(jnp.bfloat16).astype(jnp.float32)
    return jnp.where(lane < 4, high, jnp.where(lane < 8, mid, rest - mid)).astype(jnp.bfloat16)


def flash_kernel(pieces, call, carry, final, *refs):
    meta = refs[0]
    q_own, q_oth = refs[1], refs[2]
    piece_refs = refs[3 : 3 + len(pieces)]
    rest = list(refs[3 + len(pieces) :])
    if carry:
        acc_in, ml_in = rest.pop(0), rest.pop(0)
    out_a, out_b = rest.pop(0), rest.pop(0)
    kt, v_s, q_s, acc, m_s, l_s = rest
    core = meta[CORE_AT]

    tile = 0
    for piece, keys in zip(piece_refs, pieces):
        for t in range(keys // 128):
            rows = pl.ds(t * 128, 128)
            kt[tile] = piece[rows, pl.ds(0, D)].T
            v_s[tile] = piece[rows, pl.ds(D, D)]
            tile += 1

    for hf in range(2):
        for h in range(4):
            rows, cols = pl.ds(hf * 128, 128), pl.ds(h * 128, 128)
            q_s[hf * 4 + h, pl.ds(0, 128), :] = q_own[rows, cols]
            q_s[hf * 4 + h, pl.ds(128, 128), :] = q_oth[rows, cols]
            if carry:
                acc[hf * 4 + h] = acc_in[hf * 4 + h]
                m_s[hf * 4 + h] = jnp.broadcast_to(ml_in[hf, :, h : h + 1], (256, 128))
                lane = lax.broadcasted_iota(jnp.int32, (256, 128), 1)
                l_s[hf * 4 + h] = jnp.where(lane == 0, ml_in[hf, :, 4 + h : 5 + h], 0.0)
            else:
                acc[hf * 4 + h] = jnp.zeros((256, 128), jnp.float32)
                m_s[hf * 4 + h] = jnp.full((256, 128), MASKED, jnp.float32)
                l_s[hf * 4 + h] = jnp.zeros((256, 128), jnp.float32)

    row = lax.broadcasted_iota(jnp.int32, (256, 128), 0)
    lane = lax.broadcasted_iota(jnp.int32, (256, 128), 1)
    own_row = row < 128
    in_half = jnp.where(own_row, row, row - 128)
    q_core = jnp.where(own_row, core, 1 - core)
    q_off = jnp.where(in_half >= 64, in_half + 64, in_half) + q_core * 64
    k_off = jnp.where(lane >= 64, lane + 64, lane) + core * 64

    def step(hf, tile_a, tile_b, masks):
        k = jnp.concatenate([kt[tile_a], kt[tile_b]], 1)
        v = jnp.concatenate([v_s[tile_a], v_s[tile_b]], 0)
        ss = [
            lax.dot_general(
                q_s[hf * 4 + h], k, (((1,), (0,)), ((), ())), preferred_element_type=jnp.float32
            )
            for h in range(4)
        ]
        ps, fades = [], []
        for h in range(4):
            i = hf * 4 + h
            s_a, s_b = ss[h][:, :128], ss[h][:, 128:]
            if masks is not None:
                s_a = jnp.where(masks[0], s_a, MASKED)
                s_b = jnp.where(masks[1], s_b, MASKED)
            old = m_s[i]
            new = jnp.maximum(old, jnp.max(jnp.maximum(s_a, s_b), axis=1, keepdims=True))
            m_s[i] = new
            p_a = jnp.exp2((s_a - new) * LOG2E_SCALE)
            p_b = jnp.exp2((s_b - new) * LOG2E_SCALE)
            fades.append(jnp.exp2((old - new) * LOG2E_SCALE))
            l_s[i] = l_s[i] * fades[-1] + p_a + p_b
            ps.append(jnp.concatenate([p_a.astype(jnp.bfloat16), p_b.astype(jnp.bfloat16)], 1))
        for h in range(4):
            i = hf * 4 + h
            acc[i] = acc[i] * fades[h] + jnp.dot(ps[h], v, preferred_element_type=jnp.float32)

    def quad(hf, tiles4):
        k = jnp.concatenate([kt[t] for t in tiles4], 1)
        v = jnp.concatenate([v_s[t] for t in tiles4], 0)
        ss = [
            lax.dot_general(
                q_s[hf * 4 + h], k, (((1,), (0,)), ((), ())), preferred_element_type=jnp.float32
            )
            for h in range(4)
        ]
        ps, fades = [], []
        for h in range(4):
            i = hf * 4 + h
            st = [ss[h][:, t * 128 : t * 128 + 128] for t in range(4)]
            top = jnp.maximum(jnp.maximum(st[0], st[1]), jnp.maximum(st[2], st[3]))
            old = m_s[i]
            new = jnp.maximum(old, jnp.max(top, axis=1, keepdims=True))
            m_s[i] = new
            p = [jnp.exp2((a - new) * LOG2E_SCALE) for a in st]
            fades.append(jnp.exp2((old - new) * LOG2E_SCALE))
            l_s[i] = l_s[i] * fades[-1] + (p[0] + p[1]) + (p[2] + p[3])
            ps.append(jnp.concatenate([a.astype(jnp.bfloat16) for a in p], 1))
        for h in range(4):
            i = hf * 4 + h
            acc[i] = acc[i] * fades[h] + jnp.dot(ps[h], v, preferred_element_type=jnp.float32)

    for hf in range(2):
        qb = meta[Q_AT + CALLS[call][0] * 2 + hf]
        off = (call * 2 + hf) * PLAN
        n_full, n_part = meta[off], meta[off + 1]

        def whole(j):
            return meta[off + 2 + j] & 255

        def whole_quad(j, _):
            quad(hf, [whole(4 * j + t) for t in range(4)])
            return 0

        lax.fori_loop(0, n_full // 4, whole_quad, 0)

        def whole_pair(j, _):
            step(hf, whole(2 * j), whole(2 * j + 1), None)
            return 0

        lax.fori_loop(n_full // 4 * 2, n_full // 2, whole_pair, 0)

        q_pos = qb + q_off
        q_lo = doc_start(meta, q_pos)

        def part_pair(j, _):
            there = 2 * j + 1 < n_part
            e_a = meta[off + 36 + 2 * j]
            e_b = jnp.where(there, meta[off + 37 + 2 * j], e_a)
            tile_a, tile_b = e_a & 255, e_b & 255
            k_a = (e_a >> 8) + k_off
            k_b = jnp.where(there, e_b >> 8, NEVER) + k_off
            masks = ((k_a <= q_pos) & (k_a >= q_lo), (k_b <= q_pos) & (k_b >= q_lo))
            step(hf, tile_a, tile_b, masks)
            return 0

        lax.fori_loop(0, (n_part + 1) // 2, part_pair, 0)

        stats = jnp.zeros((256, 128), jnp.float32)
        rows = pl.ds(hf * 128, 128)
        for h in range(4):
            i, cols = hf * 4 + h, pl.ds(h * 128, 128)
            total = jnp.sum(l_s[i], axis=1, keepdims=True)
            if final:
                total = jnp.maximum(total, 1e-30)
                log_sum = m_s[i] * LOG2E_SCALE + jnp.log2(total)
                stats = jnp.where((lane % 4 == h) & (lane < 12), log_sum, stats)
                mean = acc[i] / total
                out_a[rows, cols] = mean[:128]
                out_b[rows, cols] = mean[128:].astype(jnp.bfloat16)
            else:
                stats = jnp.where(lane == h, m_s[i], stats)
                stats = jnp.where(lane == 4 + h, total, stats)
                out_a[i] = acc[i]
        if final:
            out_a[rows, pl.ds(512, 128)] = stats[:128]
            out_b[rows, pl.ds(512, 128)] = three_parts(stats[128:])
        else:
            out_b[hf] = stats


def flash(meta, q_own, q_oth, pieces, call, state, final):
    rows = tuple(p.shape[0] for p in pieces)
    carry = state is not None
    keys = sum(rows)
    if final:
        shapes = [jax.ShapeDtypeStruct((256, 640), t) for t in (jnp.float32, jnp.bfloat16)]
    else:
        shapes = [
            jax.ShapeDtypeStruct((8, 256, 128), jnp.float32),
            jax.ShapeDtypeStruct((2, 256, 128), jnp.float32),
        ]
    vmem = pl.BlockSpec(memory_space=pltpu.VMEM)
    in_specs = [pl.BlockSpec(memory_space=pltpu.SMEM), vmem, vmem]
    in_specs += [vmem] * (len(pieces) + (2 if carry else 0))
    return pl.pallas_call(
        functools.partial(flash_kernel, rows, call, carry, final),
        out_shape=shapes,
        in_specs=in_specs,
        out_specs=[vmem, vmem],
        scratch_shapes=[
            pltpu.VMEM((keys // 128, 128, 128), jnp.bfloat16),
            pltpu.VMEM((keys // 128, 128, 128), jnp.bfloat16),
            pltpu.VMEM((8, 256, 128), jnp.bfloat16),
            pltpu.VMEM((8, 256, 128), jnp.float32),
            pltpu.VMEM((8, 256, 128), jnp.float32),
            pltpu.VMEM((8, 256, 128), jnp.float32),
        ],
        compiler_params=pltpu.CompilerParams(vmem_limit_bytes=VMEM_LIMIT),
        cost_estimate=pl.CostEstimate(
            flops=CALLS[call][3] * 2048 * keys * D, bytes_accessed=keys * 512, transcendentals=0
        ),
        name="flash",
    )(meta, q_own, q_oth, *pieces, *(state if carry else ()))


def merge_kernel(count, *refs):
    ins, outs = refs[:count], refs[count:]
    step = 256 // len(outs)
    for s, out in enumerate(outs):
        at = lax.rem(my_z() + s, 4) * 64 if len(outs) == 4 else 0
        rows = pl.ds(pl.multiple_of(at, 64), step)
        logs = []
        for a in ins:
            log_sum = a[rows, pl.ds(512, 128)].astype(jnp.float32)
            if a.dtype == jnp.bfloat16:
                log_sum = log_sum[:, 0:4] + log_sum[:, 4:8] + log_sum[:, 8:12]
            logs.append(log_sum[:, 0:4])
        top = functools.reduce(jnp.maximum, logs)
        weights = [jnp.exp2(log_sum - top) for log_sum in logs]
        total = sum(weights)
        weights = [w / total for w in weights]
        for h in range(4):
            cols = pl.ds(h * 128, 128)
            mixed = sum(
                a[rows, cols].astype(jnp.float32) * w[:, h : h + 1] for a, w in zip(ins, weights)
            )
            out[:, cols] = mixed.astype(jnp.bfloat16)
        if len(outs) == 1:
            log_sum = top + jnp.log2(total)
            lane = lax.broadcasted_iota(jnp.int32, (step, 128), 1)
            spread = jnp.zeros((step, 128), jnp.float32)
            for h in range(4):
                spread = jnp.where((lane % 4 == h) & (lane < 12), log_sum[:, h : h + 1], spread)
            out[:, pl.ds(512, 128)] = three_parts(spread)


def merge(partials, last):
    vmem = pl.BlockSpec(memory_space=pltpu.VMEM)
    shape, count = ((64, 512), 4) if last else ((256, 640), 1)
    return pl.pallas_call(
        functools.partial(merge_kernel, len(partials)),
        out_shape=[jax.ShapeDtypeStruct(shape, jnp.bfloat16)] * count,
        in_specs=[vmem] * len(partials),
        out_specs=[vmem] * count,
        compiler_params=pltpu.CompilerParams(vmem_limit_bytes=SMALL_LIMIT),
        name="merge",
    )(*partials)


def other_core(zl, x, y, zh, c):
    return (zl, x, y, zh, c + 1)


def other_lo(zl, x, y, zh, c):
    return (zl + 1, x, y, zh, c)


def after(first, *then):
    return lax.optimization_barrier((first, *then))[1:]


def local(queries, keys, values, position, segment):
    with jax.named_scope("heads"):
        parts = pack(keys.reshape(64, 512), values.reshape(64, 512), queries.reshape(64, 2048))
        kv, q_own = unpack(over_z(parts), (256, 512))
    with jax.named_scope("plan"):
        plan = make_plan(position, segment, kv[:16, :128])
    with jax.named_scope("kv_first"):
        line = [kv] + [send(kv, along(True, step)) for step in (1, -1, 2)]
        line = after(plan, *line)
        line = jnp.concatenate(line, 0)
    with jax.named_scope("q_other"):
        far_own = send(q_own, other_lo)
        q_oth = send(*after(line, q_own), other_core)
    with jax.named_scope("kv_second"):
        up, down = send(line, along(False, 1)), send(line, along(False, -1))
        half_a, half_b = send(up[:512], along(False, 1)), send(down[512:], along(False, -1))
    with jax.named_scope("attend_far"):
        (far_own,) = after(up, far_own)
        far_oth = send(far_own, other_core)
        keys = [line, up, down, half_a, half_b]
        mine, theirs = flash(plan, far_own, far_oth, keys, 0, None, True)
    with jax.named_scope("merge_far"):
        (far,) = merge([mine, send(theirs, other_core)], False)
        far_got = send(far, other_lo)
    with jax.named_scope("attend_own"):
        q_own, q_oth = after(far, q_own, q_oth)
        mine, theirs = flash(plan, q_own, q_oth, keys, 1, None, True)
    with jax.named_scope("merge_own"):
        (theirs,) = after(far_got, theirs)
        parts = merge([mine, send(theirs, other_core), far_got], True)
    with jax.named_scope("out_heads"):
        out = finish(over_z(parts))
    return out.reshape(1, 64, HEADS * D)


def solution(mesh):
    spec = P("blk", "head", None)
    return jax.shard_map(
        local,
        mesh=mesh,
        in_specs=(spec, spec, spec, P(), P()),
        out_specs=spec,
        check_vma=False,
    )
```

```python
import functools

import jax
import jax.numpy as jnp
import numpy as np
from jax import lax
from jax.experimental import pallas as pl
from jax.experimental.pallas import tpu as pltpu
from jax.sharding import PartitionSpec as P

HEADS = 16
KV = 4
D = 128
AXES = ("head", "blk")
NEVER = 1 << 20
MASKED = -1e30
LOG2E_SCALE = float(np.log2(np.e) * D**-0.5)
VMEM_LIMIT = 32 * 1024 * 1024
SMALL_LIMIT = 8 * 1024 * 1024


def device_of(zl, x, y, zh, c):
    return ((zh % 4) * 2 + c % 2) * 32 + (zl % 2) * 16 + (x % 4) * 4 + y % 4


def place_of(device):
    h, b = device // 32, device % 32
    return b // 16, (b // 4) % 4, b % 4, h // 2, h % 2


def send(a, to):
    pairs = [(i, device_of(*to(*place_of(i)))) for i in range(256)]
    return lax.ppermute(a, AXES, pairs)


def along(first, step):
    def to(zl, x, y, zh, c):
        on_x = (c == 0) == first
        return (zl, x + step, y, zh, c) if on_x else (zl, x, y + step, zh, c)

    return to


SHIFTS = (0, 3, 1, 2)


def my_z():
    return lax.axis_index("head") // 2


def cut(arrays, s):
    head, at = lax.rem(my_z() + s, 4), 0
    for a in arrays:
        width = a.shape[1] // 4
        yield a, pl.ds(pl.multiple_of(head * width, width), width), at
        at += width


def pack_kernel(*refs):
    ins, outs, sems = refs[:3], refs[3:6], refs[6]
    copies = []
    for s, out in enumerate(outs):
        for i, (a, cols, at) in enumerate(cut(ins, s + 1)):
            width = a.shape[1] // 4
            copy = pltpu.make_async_copy(a.at[:, cols], out.at[:, pl.ds(at, width)], sems.at[s, i])
            copy.start()
            copies.append(copy)
    for copy in copies:
        copy.wait()


def pack(*arrays):
    width = sum(a.shape[1] for a in arrays) // 4
    vmem = pl.BlockSpec(memory_space=pltpu.VMEM)
    return pl.pallas_call(
        pack_kernel,
        out_shape=[jax.ShapeDtypeStruct((64, width), jnp.bfloat16)] * 3,
        in_specs=[pl.BlockSpec(memory_space=pl.ANY)] * 3,
        out_specs=[vmem] * 3,
        scratch_shapes=[pltpu.SemaphoreType.DMA((3, 3))],
        name="pack",
    )(*arrays)


def unpack_kernel(*refs):
    ins, outs = refs[:3], refs[6:]
    own = pl.ds(pl.multiple_of(my_z() * 64, 64), 64)
    for a, cols, at in cut(ins, 0):
        width = a.shape[1] // 4
        if at < 256:
            outs[0][own, pl.ds(at, width)] = a[:, cols]
        else:
            outs[1][own, :] = a[:, cols]
    for s in range(1, 4):
        rows = pl.ds(pl.multiple_of(lax.rem(my_z() + 4 - s, 4) * 64, 64), 64)
        outs[0][rows, :] = refs[2 + s][:, pl.ds(0, 256)]
        outs[1][rows, :] = refs[2 + s][:, pl.ds(256, 512)]


def unpack(arrays, got):
    vmem = pl.BlockSpec(memory_space=pltpu.VMEM)
    return pl.pallas_call(
        unpack_kernel,
        out_shape=[jax.ShapeDtypeStruct((256, w), jnp.bfloat16) for w in (256, 512)],
        in_specs=[vmem] * 6,
        out_specs=[vmem] * 2,
        compiler_params=pltpu.CompilerParams(vmem_limit_bytes=SMALL_LIMIT),
        name="unpack",
    )(*arrays, *got)


def finish_kernel(*refs):
    for s in range(4):
        z = lax.rem(my_z() + 4 - s, 4)
        refs[4][:, pl.ds(pl.multiple_of(z * 512, 512), 512)] = refs[s][...]


def finish(arrays):
    vmem = pl.BlockSpec(memory_space=pltpu.VMEM)
    return pl.pallas_call(
        finish_kernel,
        out_shape=jax.ShapeDtypeStruct((64, HEADS * D), jnp.bfloat16),
        in_specs=[vmem] * 4,
        out_specs=vmem,
        compiler_params=pltpu.CompilerParams(vmem_limit_bytes=SMALL_LIMIT),
        name="finish",
    )(*arrays)


def over_z(arrays):
    return [
        send(a, lambda zl, x, y, z, c, s=s: (zl, x, y, z + s, c)) for s, a in enumerate(arrays, 1)
    ]


CALLS = ((1, 0, 12, 1), (1, 12, 4, 1), (0, 0, 16, 24))
PLAN = 72
Q_AT = 2 * len(CALLS) * PLAN
CORE_AT = Q_AT + 4
EDGE_AT = Q_AT + 5


def doc_start(meta, at):
    start = jnp.zeros_like(at)
    for s in range(3):
        edge = meta[EDGE_AT + s]
        start = jnp.maximum(start, jnp.where(edge <= at, edge, 0))
    return start


def plan_kernel(pos_hbm, seg_hbm, plan, first_ref, pos_ref, seg_ref, sems):
    core, block = lax.rem(lax.axis_index("head"), 2), lax.axis_index("blk")
    runs = [
        pltpu.make_async_copy(pos_hbm.at[:, pl.ds(h * 256, 128)], first_ref.at[h], sems.at[h])
        for h in range(2)
    ]
    whole = [
        pltpu.make_async_copy(pos_hbm, pos_ref, sems.at[2]),
        pltpu.make_async_copy(seg_hbm, seg_ref, sems.at[3]),
    ]
    for copy in whole + runs:
        copy.start()
    for copy in whole:
        copy.wait()
    zl, x, y = block // 16, (block // 4) % 4, block % 4
    pos, seg = pos_ref[...], seg_ref[...]
    for s in range(1, 4):
        plan[EDGE_AT + s - 1] = jnp.min(jnp.where(seg >= s, pos, NEVER))
    plan[CORE_AT] = core
    for copy in runs:
        copy.wait()
    queries = []
    for whose in range(2):
        for hf in range(2):
            qb = first_ref[hf, (block + 16 * whose) % 32, 0]
            plan[Q_AT + whose * 2 + hf] = qb
            queries.append((qb, doc_start(plan, qb), doc_start(plan, qb + 255)))
    for call, (whose, first, blocks, _) in enumerate(CALLS):
        counts = [[jnp.int32(0), jnp.int32(0)] for _ in range(2)]
        for k in range(first, first + blocks):
            s1, s2 = SHIFTS[k % 4], SHIFTS[k // 4]
            on_x, on_y = jnp.where(core == 0, s1, s2), jnp.where(core == 0, s2, s1)
            source = zl * 16 + (x + on_x) % 4 * 4 + (y + on_y) % 4
            for t in range(2):
                kb = first_ref[t, source, 0]
                entry = ((k - first) * 2 + t) + kb * 256
                for hf in range(2):
                    off = (call * 2 + hf) * PLAN
                    qb, lo_first, lo_last = queries[whose * 2 + hf]
                    n_full, n_part = counts[hf]
                    seen = (kb <= qb) & (kb + 255 >= lo_first)
                    whole = seen & (kb < qb) & (kb >= lo_last)
                    plan[off + 2 + n_full] = entry
                    plan[off + 36 + n_part] = entry
                    counts[hf][0] = n_full + jnp.where(whole, 1, 0)
                    counts[hf][1] = n_part + jnp.where(seen & jnp.logical_not(whole), 1, 0)
        for hf in range(2):
            off = (call * 2 + hf) * PLAN
            n_full, n_part = counts[hf]
            odd = n_full % 2
            last = plan[off + 2 + jnp.maximum(n_full - 1, 0)]
            plan[off + 36 + n_part] = jnp.where(odd == 1, last, plan[off + 36 + n_part])
            plan[off] = n_full
            plan[off + 1] = n_part + odd


def make_plan(position, segment):
    return pl.pallas_call(
        plan_kernel,
        out_shape=jax.ShapeDtypeStruct((EDGE_AT + 3,), jnp.int32),
        in_specs=[pl.BlockSpec(memory_space=pl.ANY)] * 2,
        out_specs=pl.BlockSpec(memory_space=pltpu.SMEM),
        scratch_shapes=[
            pltpu.SMEM((2, 32, 128), jnp.int32),
            pltpu.VMEM((32, 512), jnp.int32),
            pltpu.VMEM((32, 512), jnp.int32),
            pltpu.SemaphoreType.DMA((4,)),
        ],
        compiler_params=pltpu.CompilerParams(vmem_limit_bytes=SMALL_LIMIT),
        name="plan",
    )(position, segment)


def three_parts(log_sum):
    lane = lax.broadcasted_iota(jnp.int32, log_sum.shape, 1)
    high = log_sum.astype(jnp.bfloat16).astype(jnp.float32)
    rest = log_sum - high
    mid = rest.astype(jnp.bfloat16).astype(jnp.float32)
    return jnp.where(lane < 4, high, jnp.where(lane < 8, mid, rest - mid)).astype(jnp.bfloat16)


def flash_kernel(pieces, call, carry, final, *refs):
    meta = refs[0]
    q_own, q_oth = refs[1], refs[2]
    piece_refs = refs[3 : 3 + len(pieces)]
    rest = list(refs[3 + len(pieces) :])
    if carry:
        acc_in, ml_in = rest.pop(0), rest.pop(0)
    out_a, out_b = rest.pop(0), rest.pop(0)
    kt, v_s, q_s, acc, m_s, l_s = rest
    core = meta[CORE_AT]

    tile = 0
    for piece, keys in zip(piece_refs, pieces):
        for t in range(keys // 128):
            rows = pl.ds(t * 128, 128)
            kt[tile] = piece[rows, pl.ds(0, D)].T
            v_s[tile] = piece[rows, pl.ds(D, D)]
            tile += 1

    for hf in range(2):
        for h in range(4):
            rows, cols = pl.ds(hf * 128, 128), pl.ds(h * 128, 128)
            q_s[hf * 4 + h, pl.ds(0, 128), :] = q_own[rows, cols]
            q_s[hf * 4 + h, pl.ds(128, 128), :] = q_oth[rows, cols]
            if carry:
                acc[hf * 4 + h] = acc_in[hf * 4 + h]
                m_s[hf * 4 + h] = jnp.broadcast_to(ml_in[hf, :, h : h + 1], (256, 128))
                lane = lax.broadcasted_iota(jnp.int32, (256, 128), 1)
                l_s[hf * 4 + h] = jnp.where(lane == 0, ml_in[hf, :, 4 + h : 5 + h], 0.0)
            else:
                acc[hf * 4 + h] = jnp.zeros((256, 128), jnp.float32)
                m_s[hf * 4 + h] = jnp.full((256, 128), MASKED, jnp.float32)
                l_s[hf * 4 + h] = jnp.zeros((256, 128), jnp.float32)

    row = lax.broadcasted_iota(jnp.int32, (256, 128), 0)
    lane = lax.broadcasted_iota(jnp.int32, (256, 128), 1)
    own_row = row < 128
    in_half = jnp.where(own_row, row, row - 128)
    q_core = jnp.where(own_row, core, 1 - core)
    q_off = jnp.where(in_half >= 64, in_half + 64, in_half) + q_core * 64
    k_off = jnp.where(lane >= 64, lane + 64, lane) + core * 64

    def step(hf, tile_a, tile_b, masks):
        k = jnp.concatenate([kt[tile_a], kt[tile_b]], 1)
        v = jnp.concatenate([v_s[tile_a], v_s[tile_b]], 0)
        ss = [
            lax.dot_general(
                q_s[hf * 4 + h], k, (((1,), (0,)), ((), ())), preferred_element_type=jnp.float32
            )
            for h in range(4)
        ]
        ps, fades = [], []
        for h in range(4):
            i = hf * 4 + h
            s_a, s_b = ss[h][:, :128], ss[h][:, 128:]
            if masks is not None:
                s_a = jnp.where(masks[0], s_a, MASKED)
                s_b = jnp.where(masks[1], s_b, MASKED)
            old = m_s[i]
            new = jnp.maximum(old, jnp.max(jnp.maximum(s_a, s_b), axis=1, keepdims=True))
            m_s[i] = new
            p_a = jnp.exp2((s_a - new) * LOG2E_SCALE)
            p_b = jnp.exp2((s_b - new) * LOG2E_SCALE)
            fades.append(jnp.exp2((old - new) * LOG2E_SCALE))
            l_s[i] = l_s[i] * fades[-1] + p_a + p_b
            ps.append(jnp.concatenate([p_a.astype(jnp.bfloat16), p_b.astype(jnp.bfloat16)], 1))
        for h in range(4):
            i = hf * 4 + h
            acc[i] = acc[i] * fades[h] + jnp.dot(ps[h], v, preferred_element_type=jnp.float32)

    def quad(hf, tiles4):
        k = jnp.concatenate([kt[t] for t in tiles4], 1)
        v = jnp.concatenate([v_s[t] for t in tiles4], 0)
        ss = [
            lax.dot_general(
                q_s[hf * 4 + h], k, (((1,), (0,)), ((), ())), preferred_element_type=jnp.float32
            )
            for h in range(4)
        ]
        ps, fades = [], []
        for h in range(4):
            i = hf * 4 + h
            st = [ss[h][:, t * 128 : t * 128 + 128] for t in range(4)]
            top = jnp.maximum(jnp.maximum(st[0], st[1]), jnp.maximum(st[2], st[3]))
            old = m_s[i]
            new = jnp.maximum(old, jnp.max(top, axis=1, keepdims=True))
            m_s[i] = new
            p = [jnp.exp2((a - new) * LOG2E_SCALE) for a in st]
            fades.append(jnp.exp2((old - new) * LOG2E_SCALE))
            l_s[i] = l_s[i] * fades[-1] + (p[0] + p[1]) + (p[2] + p[3])
            ps.append(jnp.concatenate([a.astype(jnp.bfloat16) for a in p], 1))
        for h in range(4):
            i = hf * 4 + h
            acc[i] = acc[i] * fades[h] + jnp.dot(ps[h], v, preferred_element_type=jnp.float32)

    for hf in range(2):
        qb = meta[Q_AT + CALLS[call][0] * 2 + hf]
        off = (call * 2 + hf) * PLAN
        n_full, n_part = meta[off], meta[off + 1]

        def whole(j):
            return meta[off + 2 + j] & 255

        def whole_quad(j, _):
            quad(hf, [whole(4 * j + t) for t in range(4)])
            return 0

        lax.fori_loop(0, n_full // 4, whole_quad, 0)

        def whole_pair(j, _):
            step(hf, whole(2 * j), whole(2 * j + 1), None)
            return 0

        lax.fori_loop(n_full // 4 * 2, n_full // 2, whole_pair, 0)

        q_pos = qb + q_off
        q_lo = doc_start(meta, q_pos)

        def part_pair(j, _):
            there = 2 * j + 1 < n_part
            e_a = meta[off + 36 + 2 * j]
            e_b = jnp.where(there, meta[off + 37 + 2 * j], e_a)
            tile_a, tile_b = e_a & 255, e_b & 255
            k_a = (e_a >> 8) + k_off
            k_b = jnp.where(there, e_b >> 8, NEVER) + k_off
            masks = ((k_a <= q_pos) & (k_a >= q_lo), (k_b <= q_pos) & (k_b >= q_lo))
            step(hf, tile_a, tile_b, masks)
            return 0

        lax.fori_loop(0, (n_part + 1) // 2, part_pair, 0)

        stats = jnp.zeros((256, 128), jnp.float32)
        rows = pl.ds(hf * 128, 128)
        for h in range(4):
            i, cols = hf * 4 + h, pl.ds(h * 128, 128)
            total = jnp.sum(l_s[i], axis=1, keepdims=True)
            if final:
                total = jnp.maximum(total, 1e-30)
                log_sum = m_s[i] * LOG2E_SCALE + jnp.log2(total)
                stats = jnp.where((lane % 4 == h) & (lane < 12), log_sum, stats)
                mean = acc[i] * (1 / total)
                out_a[rows, cols] = mean[:128]
                out_b[rows, cols] = mean[128:].astype(jnp.bfloat16)
            else:
                stats = jnp.where(lane == h, m_s[i], stats)
                stats = jnp.where(lane == 4 + h, total, stats)
                out_a[i] = acc[i]
        if final:
            out_a[rows, pl.ds(512, 128)] = stats[:128]
            out_b[rows, pl.ds(512, 128)] = three_parts(stats[128:])
        else:
            out_b[hf] = stats


def flash(meta, q_own, q_oth, pieces, call, state, final):
    rows = tuple(p.shape[0] for p in pieces)
    carry = state is not None
    keys = sum(rows)
    if final:
        shapes = [jax.ShapeDtypeStruct((256, 640), t) for t in (jnp.float32, jnp.bfloat16)]
    else:
        shapes = [
            jax.ShapeDtypeStruct((8, 256, 128), jnp.float32),
            jax.ShapeDtypeStruct((2, 256, 128), jnp.float32),
        ]
    vmem = pl.BlockSpec(memory_space=pltpu.VMEM)
    in_specs = [pl.BlockSpec(memory_space=pltpu.SMEM), vmem, vmem]
    in_specs += [vmem] * (len(pieces) + (2 if carry else 0))
    return pl.pallas_call(
        functools.partial(flash_kernel, rows, call, carry, final),
        out_shape=shapes,
        in_specs=in_specs,
        out_specs=[vmem, vmem],
        scratch_shapes=[
            pltpu.VMEM((keys // 128, 128, 128), jnp.bfloat16),
            pltpu.VMEM((keys // 128, 128, 128), jnp.bfloat16),
            pltpu.VMEM((8, 256, 128), jnp.bfloat16),
            pltpu.VMEM((8, 256, 128), jnp.float32),
            pltpu.VMEM((8, 256, 128), jnp.float32),
            pltpu.VMEM((8, 256, 128), jnp.float32),
        ],
        compiler_params=pltpu.CompilerParams(vmem_limit_bytes=VMEM_LIMIT),
        cost_estimate=pl.CostEstimate(
            flops=CALLS[call][3] * 2048 * keys * D, bytes_accessed=keys * 512, transcendentals=0
        ),
        name="flash",
    )(meta, q_own, q_oth, *pieces, *(state if carry else ()))


def merge_kernel(count, *refs):
    ins, outs = refs[:count], refs[count:]
    step = 256 // len(outs)
    for s, out in enumerate(outs):
        at = lax.rem(my_z() + s, 4) * 64 if len(outs) == 4 else 0
        rows = pl.ds(pl.multiple_of(at, 64), step)
        logs = []
        for a in ins:
            log_sum = a[rows, pl.ds(512, 128)].astype(jnp.float32)
            if a.dtype == jnp.bfloat16:
                log_sum = log_sum[:, 0:4] + log_sum[:, 4:8] + log_sum[:, 8:12]
            logs.append(log_sum[:, 0:4])
        top = functools.reduce(jnp.maximum, logs)
        weights = [jnp.exp2(log_sum - top) for log_sum in logs]
        total = sum(weights)
        weights = [w / total for w in weights]
        for h in range(4):
            cols = pl.ds(h * 128, 128)
            mixed = sum(
                a[rows, cols].astype(jnp.float32) * w[:, h : h + 1] for a, w in zip(ins, weights)
            )
            out[:, cols] = mixed.astype(jnp.bfloat16)
        if len(outs) == 1:
            log_sum = top + jnp.log2(total)
            lane = lax.broadcasted_iota(jnp.int32, (step, 128), 1)
            spread = jnp.zeros((step, 128), jnp.float32)
            for h in range(4):
                spread = jnp.where((lane % 4 == h) & (lane < 12), log_sum[:, h : h + 1], spread)
            out[:, pl.ds(512, 128)] = three_parts(spread)


def merge(partials, last):
    vmem = pl.BlockSpec(memory_space=pltpu.VMEM)
    shape, count = ((64, 512), 4) if last else ((256, 640), 1)
    return pl.pallas_call(
        functools.partial(merge_kernel, len(partials)),
        out_shape=[jax.ShapeDtypeStruct(shape, jnp.bfloat16)] * count,
        in_specs=[vmem] * len(partials),
        out_specs=[vmem] * count,
        compiler_params=pltpu.CompilerParams(vmem_limit_bytes=SMALL_LIMIT),
        name="merge",
    )(*partials)


def other_core(zl, x, y, zh, c):
    return (zl, x, y, zh, c + 1)


def other_lo(zl, x, y, zh, c):
    return (zl + 1, x, y, zh, c)


def after(first, *then):
    return lax.optimization_barrier((first, *then))[1:]


def local(queries, keys, values, position, segment):
    with jax.named_scope("heads"):
        held = keys.reshape(64, 512), values.reshape(64, 512), queries.reshape(64, 2048)
        plan = make_plan(position, segment)
        kv, q_own = unpack(held, after(plan, *over_z(pack(*held))))
    with jax.named_scope("kv_first"):
        line = [kv] + [send(kv, along(True, step)) for step in (1, -1, 2)]
        line_a, line_b = jnp.concatenate(line[:2], 0), jnp.concatenate(line[2:], 0)
    with jax.named_scope("kv_second"):
        up_a, down_b = send(line_a, along(False, 1)), send(line_b, along(False, -1))
        up_b, down_a = send(line_b, along(False, 1)), send(line_a, along(False, -1))
        far_a, far_b = send(up_a, along(False, 1)), send(down_b, along(False, -1))
    with jax.named_scope("q_other"):
        q_oth = send(*after(line_a, q_own), other_core)
        far_own = send(q_own, other_lo)
        (far_own,) = after(up_b, far_own)
        far_oth = send(far_own, other_core)
    with jax.named_scope("attend_far"):
        keys = [line_a, line_b, up_a, up_b, down_a, down_b, far_a, far_b]
        state = flash(plan, far_own, far_oth, keys[:6], 0, None, False)
        mine, theirs = flash(plan, far_own, far_oth, keys[6:], 1, state, True)
    with jax.named_scope("merge_far"):
        (far,) = merge([mine, send(theirs, other_core)], False)
        far_got = send(far, other_lo)
    with jax.named_scope("attend_own"):
        q_own, q_oth = after(far, q_own, q_oth)
        mine, theirs = flash(plan, q_own, q_oth, keys, 2, None, True)
    with jax.named_scope("merge_own"):
        (theirs,) = after(far_got, theirs)
        parts = merge([mine, send(theirs, other_core), far_got], True)
    with jax.named_scope("out_heads"):
        out = finish([parts[0]] + over_z(parts[1:]))
    return out.reshape(1, 64, HEADS * D)


def solution(mesh):
    spec = P("blk", "head", None)
    return jax.shard_map(
        local,
        mesh=mesh,
        in_specs=(spec, spec, spec, P(), P()),
        out_specs=spec,
        check_vma=False,
    )
```

```python
import functools

import jax
import jax.numpy as jnp
import numpy as np
from jax import lax
from jax.experimental import pallas as pl
from jax.experimental.pallas import tpu as pltpu
from jax.sharding import PartitionSpec as P

HEADS = 16
KV = 4
D = 128
AXES = ("head", "blk")
NEVER = 1 << 20
MASKED = -1e30
LOG2E_SCALE = float(np.log2(np.e) * D**-0.5)
VMEM_LIMIT = 32 * 1024 * 1024
SMALL_LIMIT = 8 * 1024 * 1024


def device_of(zl, x, y, zh, c):
    return ((zh % 4) * 2 + c % 2) * 32 + (zl % 2) * 16 + (x % 4) * 4 + y % 4


def place_of(device):
    h, b = device // 32, device % 32
    return b // 16, (b // 4) % 4, b % 4, h // 2, h % 2


def send(a, to):
    pairs = [(i, device_of(*to(*place_of(i)))) for i in range(256)]
    return lax.ppermute(a, AXES, pairs)


def along(first, step):
    def to(zl, x, y, zh, c):
        on_x = (c == 0) == first
        return (zl, x + step, y, zh, c) if on_x else (zl, x, y + step, zh, c)

    return to


SHIFTS = (0, 3, 1, 2)


def my_z():
    return lax.axis_index("head") // 2


def cut(arrays, s):
    head, at = lax.rem(my_z() + s, 4), 0
    for a in arrays:
        width = a.shape[1] // 4
        yield a, pl.ds(pl.multiple_of(head * width, width), width), at
        at += width


def pack_kernel(*refs):
    ins, outs, sems = refs[:3], refs[3:6], refs[6]
    copies = []
    for s, out in enumerate(outs):
        for i, (a, cols, at) in enumerate(cut(ins, s + 1)):
            width = a.shape[1] // 4
            copy = pltpu.make_async_copy(a.at[:, cols], out.at[:, pl.ds(at, width)], sems.at[s, i])
            copy.start()
            copies.append(copy)
    for copy in copies:
        copy.wait()


def pack(*arrays):
    width = sum(a.shape[1] for a in arrays) // 4
    vmem = pl.BlockSpec(memory_space=pltpu.VMEM)
    return pl.pallas_call(
        pack_kernel,
        out_shape=[jax.ShapeDtypeStruct((64, width), jnp.bfloat16)] * 3,
        in_specs=[pl.BlockSpec(memory_space=pl.ANY)] * 3,
        out_specs=[vmem] * 3,
        scratch_shapes=[pltpu.SemaphoreType.DMA((3, 3))],
        name="pack",
    )(*arrays)


def unpack_kernel(*refs):
    ins, outs = refs[:3], refs[6:]
    own = pl.ds(pl.multiple_of(my_z() * 64, 64), 64)
    for a, cols, at in cut(ins, 0):
        width = a.shape[1] // 4
        if at < 256:
            outs[0][own, pl.ds(at, width)] = a[:, cols]
        else:
            outs[1][own, :] = a[:, cols]
    for s in range(1, 4):
        rows = pl.ds(pl.multiple_of(lax.rem(my_z() + 4 - s, 4) * 64, 64), 64)
        outs[0][rows, :] = refs[2 + s][:, pl.ds(0, 256)]
        outs[1][rows, :] = refs[2 + s][:, pl.ds(256, 512)]


def unpack(arrays, got):
    vmem = pl.BlockSpec(memory_space=pltpu.VMEM)
    return pl.pallas_call(
        unpack_kernel,
        out_shape=[jax.ShapeDtypeStruct((256, w), jnp.bfloat16) for w in (256, 512)],
        in_specs=[vmem] * 6,
        out_specs=[vmem] * 2,
        compiler_params=pltpu.CompilerParams(vmem_limit_bytes=SMALL_LIMIT),
        name="unpack",
    )(*arrays, *got)


def finish_kernel(*refs):
    for s in range(4):
        z = lax.rem(my_z() + 4 - s, 4)
        refs[4][:, pl.ds(pl.multiple_of(z * 512, 512), 512)] = refs[s][...]


def finish(arrays):
    vmem = pl.BlockSpec(memory_space=pltpu.VMEM)
    return pl.pallas_call(
        finish_kernel,
        out_shape=jax.ShapeDtypeStruct((64, HEADS * D), jnp.bfloat16),
        in_specs=[vmem] * 4,
        out_specs=vmem,
        compiler_params=pltpu.CompilerParams(vmem_limit_bytes=SMALL_LIMIT),
        name="finish",
    )(*arrays)


def over_z(arrays):
    return [
        send(a, lambda zl, x, y, z, c, s=s: (zl, x, y, z + s, c)) for s, a in enumerate(arrays, 1)
    ]


CALLS = ((1, 0, 12, 1, False), (1, 12, 4, 1, True), (0, 0, 16, 24, False))
PLAN = 72
Q_AT = 2 * len(CALLS) * PLAN
CORE_AT = Q_AT + 4
EDGE_AT = Q_AT + 5


def doc_start(meta, at):
    start = jnp.zeros_like(at)
    for s in range(3):
        edge = meta[EDGE_AT + s]
        start = jnp.maximum(start, jnp.where(edge <= at, edge, 0))
    return start


def plan_kernel(pos_hbm, seg_hbm, plan, first_ref, pos_ref, seg_ref, sems):
    core, block = lax.rem(lax.axis_index("head"), 2), lax.axis_index("blk")
    runs = [
        pltpu.make_async_copy(pos_hbm.at[:, pl.ds(h * 256, 128)], first_ref.at[h], sems.at[h])
        for h in range(2)
    ]
    whole = [
        pltpu.make_async_copy(pos_hbm, pos_ref, sems.at[2]),
        pltpu.make_async_copy(seg_hbm, seg_ref, sems.at[3]),
    ]
    for copy in whole + runs:
        copy.start()
    for copy in whole:
        copy.wait()
    zl, x, y = block // 16, (block // 4) % 4, block % 4
    pos, seg = pos_ref[...], seg_ref[...]
    for s in range(1, 4):
        plan[EDGE_AT + s - 1] = jnp.min(jnp.where(seg >= s, pos, NEVER))
    plan[CORE_AT] = core
    for copy in runs:
        copy.wait()
    queries = []
    for whose in range(2):
        for hf in range(2):
            qb = first_ref[hf, (block + 16 * whose) % 32, 0]
            plan[Q_AT + whose * 2 + hf] = qb
            queries.append((qb, doc_start(plan, qb), doc_start(plan, qb + 255)))
    for call, (whose, first, blocks, _, carry) in enumerate(CALLS):
        counts = [[jnp.int32(0), jnp.int32(0)] for _ in range(2)]
        for k in range(first, first + blocks):
            s1, s2 = SHIFTS[k % 4], SHIFTS[k // 4]
            on_x, on_y = jnp.where(core == 0, s1, s2), jnp.where(core == 0, s2, s1)
            source = zl * 16 + (x + on_x) % 4 * 4 + (y + on_y) % 4
            for t in range(2):
                kb = first_ref[t, source, 0]
                entry = ((k - first) * 2 + t) + kb * 256
                for hf in range(2):
                    off = (call * 2 + hf) * PLAN
                    qb, lo_first, lo_last = queries[whose * 2 + hf]
                    n_full, n_part = counts[hf]
                    seen = (kb <= qb) & (kb + 255 >= lo_first)
                    whole = seen & (kb < qb) & (kb >= (lo_last if carry else lo_first))
                    plan[off + 2 + n_full] = entry
                    plan[off + 36 + n_part] = entry
                    counts[hf][0] = n_full + jnp.where(whole, 1, 0)
                    counts[hf][1] = n_part + jnp.where(seen & jnp.logical_not(whole), 1, 0)
        for hf in range(2):
            off = (call * 2 + hf) * PLAN
            n_full, n_part = counts[hf]
            odd = n_full % 2
            last = plan[off + 2 + jnp.maximum(n_full - 1, 0)]
            plan[off + 36 + n_part] = jnp.where(odd == 1, last, plan[off + 36 + n_part])
            plan[off] = n_full
            plan[off + 1] = n_part + odd


def make_plan(position, segment):
    return pl.pallas_call(
        plan_kernel,
        out_shape=jax.ShapeDtypeStruct((EDGE_AT + 3,), jnp.int32),
        in_specs=[pl.BlockSpec(memory_space=pl.ANY)] * 2,
        out_specs=pl.BlockSpec(memory_space=pltpu.SMEM),
        scratch_shapes=[
            pltpu.SMEM((2, 32, 128), jnp.int32),
            pltpu.VMEM((32, 512), jnp.int32),
            pltpu.VMEM((32, 512), jnp.int32),
            pltpu.SemaphoreType.DMA((4,)),
        ],
        compiler_params=pltpu.CompilerParams(vmem_limit_bytes=SMALL_LIMIT),
        name="plan",
    )(position, segment)


def three_parts(log_sum):
    lane = lax.broadcasted_iota(jnp.int32, log_sum.shape, 1)
    high = log_sum.astype(jnp.bfloat16).astype(jnp.float32)
    rest = log_sum - high
    mid = rest.astype(jnp.bfloat16).astype(jnp.float32)
    return jnp.where(lane < 4, high, jnp.where(lane < 8, mid, rest - mid)).astype(jnp.bfloat16)


def flash_kernel(pieces, call, carry, final, *refs):
    meta = refs[0]
    q_own, q_oth = refs[1], refs[2]
    piece_refs = refs[3 : 3 + len(pieces)]
    rest = list(refs[3 + len(pieces) :])
    if carry:
        acc_in, ml_in = rest.pop(0), rest.pop(0)
    out_a, out_b = rest.pop(0), rest.pop(0)
    kt, v_s, q_s, acc, m_s, l_s = rest
    core = meta[CORE_AT]

    tile = 0
    for piece, keys in zip(piece_refs, pieces):
        for t in range(keys // 128):
            rows = pl.ds(t * 128, 128)
            kt[tile] = piece[rows, pl.ds(0, D)].T
            v_s[tile] = piece[rows, pl.ds(D, D)]
            tile += 1

    for hf in range(2):
        for h in range(4):
            rows, cols = pl.ds(hf * 128, 128), pl.ds(h * 128, 128)
            q_s[hf * 4 + h, pl.ds(0, 128), :] = q_own[rows, cols]
            q_s[hf * 4 + h, pl.ds(128, 128), :] = q_oth[rows, cols]
            if carry:
                acc[hf * 4 + h] = acc_in[hf * 4 + h]
                m_s[hf * 4 + h] = jnp.broadcast_to(ml_in[hf, :, h : h + 1], (256, 128))
                lane = lax.broadcasted_iota(jnp.int32, (256, 128), 1)
                l_s[hf * 4 + h] = jnp.where(lane == 0, ml_in[hf, :, 4 + h : 5 + h], 0.0)
            else:
                acc[hf * 4 + h] = jnp.zeros((256, 128), jnp.float32)
                m_s[hf * 4 + h] = jnp.full((256, 128), MASKED, jnp.float32)
                l_s[hf * 4 + h] = jnp.zeros((256, 128), jnp.float32)

    row = lax.broadcasted_iota(jnp.int32, (256, 128), 0)
    lane = lax.broadcasted_iota(jnp.int32, (256, 128), 1)
    own_row = row < 128
    in_half = jnp.where(own_row, row, row - 128)
    q_core = jnp.where(own_row, core, 1 - core)
    q_off = jnp.where(in_half >= 64, in_half + 64, in_half) + q_core * 64
    k_off = jnp.where(lane >= 64, lane + 64, lane) + core * 64

    def step(hf, tile_a, tile_b, masks):
        k = jnp.concatenate([kt[tile_a], kt[tile_b]], 1)
        v = jnp.concatenate([v_s[tile_a], v_s[tile_b]], 0)
        ss = [
            lax.dot_general(
                q_s[hf * 4 + h], k, (((1,), (0,)), ((), ())), preferred_element_type=jnp.float32
            )
            for h in range(4)
        ]
        ps, fades = [], []
        for h in range(4):
            i = hf * 4 + h
            s_a, s_b = ss[h][:, :128], ss[h][:, 128:]
            if masks is not None:
                s_a = jnp.where(masks[0], s_a, MASKED)
                s_b = jnp.where(masks[1], s_b, MASKED)
            old = m_s[i]
            new = jnp.maximum(old, jnp.max(jnp.maximum(s_a, s_b), axis=1, keepdims=True))
            m_s[i] = new
            p_a = jnp.exp2((s_a - new) * LOG2E_SCALE)
            p_b = jnp.exp2((s_b - new) * LOG2E_SCALE)
            fades.append(jnp.exp2((old - new) * LOG2E_SCALE))
            l_s[i] = l_s[i] * fades[-1] + p_a + p_b
            ps.append(jnp.concatenate([p_a.astype(jnp.bfloat16), p_b.astype(jnp.bfloat16)], 1))
        for h in range(4):
            i = hf * 4 + h
            acc[i] = acc[i] * fades[h] + jnp.dot(ps[h], v, preferred_element_type=jnp.float32)

    def quad(hf, tiles4):
        k = jnp.concatenate([kt[t] for t in tiles4], 1)
        v = jnp.concatenate([v_s[t] for t in tiles4], 0)
        ss = [
            lax.dot_general(
                q_s[hf * 4 + h], k, (((1,), (0,)), ((), ())), preferred_element_type=jnp.float32
            )
            for h in range(4)
        ]
        ps, fades = [], []
        for h in range(4):
            i = hf * 4 + h
            st = [ss[h][:, t * 128 : t * 128 + 128] for t in range(4)]
            top = jnp.maximum(jnp.maximum(st[0], st[1]), jnp.maximum(st[2], st[3]))
            old = m_s[i]
            new = jnp.maximum(old, jnp.max(top, axis=1, keepdims=True))
            m_s[i] = new
            p = [jnp.exp2((a - new) * LOG2E_SCALE) for a in st]
            fades.append(jnp.exp2((old - new) * LOG2E_SCALE))
            l_s[i] = l_s[i] * fades[-1] + (p[0] + p[1]) + (p[2] + p[3])
            ps.append(jnp.concatenate([a.astype(jnp.bfloat16) for a in p], 1))
        for h in range(4):
            i = hf * 4 + h
            acc[i] = acc[i] * fades[h] + jnp.dot(ps[h], v, preferred_element_type=jnp.float32)

    for hf in range(2):
        qb = meta[Q_AT + CALLS[call][0] * 2 + hf]
        off = (call * 2 + hf) * PLAN
        n_full, n_part = meta[off], meta[off + 1]

        def whole(j):
            return meta[off + 2 + j] & 255

        def whole_quad(j, _):
            quad(hf, [whole(4 * j + t) for t in range(4)])
            return 0

        lax.fori_loop(0, n_full // 4, whole_quad, 0)

        def whole_pair(j, _):
            step(hf, whole(2 * j), whole(2 * j + 1), None)
            return 0

        lax.fori_loop(n_full // 4 * 2, n_full // 2, whole_pair, 0)

        q_pos = qb + q_off
        q_lo = doc_start(meta, q_pos)
        if not carry:

            @pl.when(doc_start(meta, qb + 255) > doc_start(meta, qb))
            def forget():
                keep = q_lo <= qb
                for h in range(4):
                    i = hf * 4 + h
                    m_s[i] = jnp.where(keep, m_s[i], MASKED)
                    l_s[i] = jnp.where(keep, l_s[i], 0.0)
                    acc[i] = jnp.where(keep, acc[i], 0.0)

        def part_pair(j, _):
            there = 2 * j + 1 < n_part
            e_a = meta[off + 36 + 2 * j]
            e_b = jnp.where(there, meta[off + 37 + 2 * j], e_a)
            tile_a, tile_b = e_a & 255, e_b & 255
            k_a = (e_a >> 8) + k_off
            k_b = jnp.where(there, e_b >> 8, NEVER) + k_off
            masks = ((k_a <= q_pos) & (k_a >= q_lo), (k_b <= q_pos) & (k_b >= q_lo))
            step(hf, tile_a, tile_b, masks)
            return 0

        lax.fori_loop(0, (n_part + 1) // 2, part_pair, 0)

        stats = jnp.zeros((256, 128), jnp.float32)
        rows = pl.ds(hf * 128, 128)
        for h in range(4):
            i, cols = hf * 4 + h, pl.ds(h * 128, 128)
            total = jnp.sum(l_s[i], axis=1, keepdims=True)
            if final:
                total = jnp.maximum(total, 1e-30)
                log_sum = m_s[i] * LOG2E_SCALE + jnp.log2(total)
                stats = jnp.where((lane % 4 == h) & (lane < 12), log_sum, stats)
                mean = acc[i] * (1 / total)
                out_a[rows, cols] = mean[:128]
                out_b[rows, cols] = mean[128:].astype(jnp.bfloat16)
            else:
                stats = jnp.where(lane == h, m_s[i], stats)
                stats = jnp.where(lane == 4 + h, total, stats)
                out_a[i] = acc[i]
        if final:
            out_a[rows, pl.ds(512, 128)] = stats[:128]
            out_b[rows, pl.ds(512, 128)] = three_parts(stats[128:])
        else:
            out_b[hf] = stats


def flash(meta, q_own, q_oth, pieces, call, state, final):
    rows = tuple(p.shape[0] for p in pieces)
    carry = state is not None
    keys = sum(rows)
    if final:
        shapes = [jax.ShapeDtypeStruct((256, 640), t) for t in (jnp.float32, jnp.bfloat16)]
    else:
        shapes = [
            jax.ShapeDtypeStruct((8, 256, 128), jnp.float32),
            jax.ShapeDtypeStruct((2, 256, 128), jnp.float32),
        ]
    vmem = pl.BlockSpec(memory_space=pltpu.VMEM)
    in_specs = [pl.BlockSpec(memory_space=pltpu.SMEM), vmem, vmem]
    in_specs += [vmem] * (len(pieces) + (2 if carry else 0))
    return pl.pallas_call(
        functools.partial(flash_kernel, rows, call, carry, final),
        out_shape=shapes,
        in_specs=in_specs,
        out_specs=[vmem, vmem],
        scratch_shapes=[
            pltpu.VMEM((keys // 128, 128, 128), jnp.bfloat16),
            pltpu.VMEM((keys // 128, 128, 128), jnp.bfloat16),
            pltpu.VMEM((8, 256, 128), jnp.bfloat16),
            pltpu.VMEM((8, 256, 128), jnp.float32),
            pltpu.VMEM((8, 256, 128), jnp.float32),
            pltpu.VMEM((8, 256, 128), jnp.float32),
        ],
        compiler_params=pltpu.CompilerParams(vmem_limit_bytes=VMEM_LIMIT),
        cost_estimate=pl.CostEstimate(
            flops=CALLS[call][3] * 2048 * keys * D, bytes_accessed=keys * 512, transcendentals=0
        ),
        name="flash",
    )(meta, q_own, q_oth, *pieces, *(state if carry else ()))


def merge_kernel(count, *refs):
    ins, outs = refs[:count], refs[count:]
    step = 256 // len(outs)
    for s, out in enumerate(outs):
        at = lax.rem(my_z() + s, 4) * 64 if len(outs) == 4 else 0
        rows = pl.ds(pl.multiple_of(at, 64), step)
        logs = []
        for a in ins:
            log_sum = a[rows, pl.ds(512, 128)].astype(jnp.float32)
            if a.dtype == jnp.bfloat16:
                log_sum = log_sum[:, 0:4] + log_sum[:, 4:8] + log_sum[:, 8:12]
            logs.append(log_sum[:, 0:4])
        top = functools.reduce(jnp.maximum, logs)
        weights = [jnp.exp2(log_sum - top) for log_sum in logs]
        total = sum(weights)
        weights = [w / total for w in weights]
        for h in range(4):
            cols = pl.ds(h * 128, 128)
            mixed = sum(
                a[rows, cols].astype(jnp.float32) * w[:, h : h + 1] for a, w in zip(ins, weights)
            )
            out[:, cols] = mixed.astype(jnp.bfloat16)
        if len(outs) == 1:
            log_sum = top + jnp.log2(total)
            lane = lax.broadcasted_iota(jnp.int32, (step, 128), 1)
            spread = jnp.zeros((step, 128), jnp.float32)
            for h in range(4):
                spread = jnp.where((lane % 4 == h) & (lane < 12), log_sum[:, h : h + 1], spread)
            out[:, pl.ds(512, 128)] = three_parts(spread)


def merge(partials, last):
    vmem = pl.BlockSpec(memory_space=pltpu.VMEM)
    shape, count = ((64, 512), 4) if last else ((256, 640), 1)
    return pl.pallas_call(
        functools.partial(merge_kernel, len(partials)),
        out_shape=[jax.ShapeDtypeStruct(shape, jnp.bfloat16)] * count,
        in_specs=[vmem] * len(partials),
        out_specs=[vmem] * count,
        compiler_params=pltpu.CompilerParams(vmem_limit_bytes=SMALL_LIMIT),
        name="merge",
    )(*partials)


def other_core(zl, x, y, zh, c):
    return (zl, x, y, zh, c + 1)


def other_lo(zl, x, y, zh, c):
    return (zl + 1, x, y, zh, c)


def after(first, *then):
    return lax.optimization_barrier((first, *then))[1:]


def local(queries, keys, values, position, segment):
    with jax.named_scope("heads"):
        held = keys.reshape(64, 512), values.reshape(64, 512), queries.reshape(64, 2048)
        plan = make_plan(position, segment)
        kv, q_own = unpack(held, after(plan, *over_z(pack(*held))))
    with jax.named_scope("kv_first"):
        line = [kv] + [send(kv, along(True, step)) for step in (1, -1, 2)]
        line_a, line_b = jnp.concatenate(line[:2], 0), jnp.concatenate(line[2:], 0)
    with jax.named_scope("kv_second"):
        up_a, down_b = send(line_a, along(False, 1)), send(line_b, along(False, -1))
        up_b, down_a = send(line_b, along(False, 1)), send(line_a, along(False, -1))
        far_a, far_b = send(up_a, along(False, 1)), send(down_b, along(False, -1))
    with jax.named_scope("q_other"):
        q_oth = send(*after(line_a, q_own), other_core)
        far_own = send(q_own, other_lo)
        (far_own,) = after(up_b, far_own)
        far_oth = send(far_own, other_core)
    with jax.named_scope("attend_far"):
        keys = [line_a, line_b, up_a, up_b, down_a, down_b, far_a, far_b]
        state = flash(plan, far_own, far_oth, keys[:6], 0, None, False)
        mine, theirs = flash(plan, far_own, far_oth, keys[6:], 1, state, True)
    with jax.named_scope("merge_far"):
        (far,) = merge([mine, send(theirs, other_core)], False)
        far_got = send(far, other_lo)
    with jax.named_scope("attend_own"):
        q_own, q_oth = after(far, q_own, q_oth)
        mine, theirs = flash(plan, q_own, q_oth, keys, 2, None, True)
    with jax.named_scope("merge_own"):
        (theirs,) = after(far_got, theirs)
        parts = merge([mine, send(theirs, other_core), far_got], True)
    with jax.named_scope("out_heads"):
        out = finish([parts[0]] + over_z(parts[1:]))
    return out.reshape(1, 64, HEADS * D)


def solution(mesh):
    spec = P("blk", "head", None)
    return jax.shard_map(
        local,
        mesh=mesh,
        in_specs=(spec, spec, spec, P(), P()),
        out_specs=spec,
        check_vma=False,
    )
```

```python
import functools

import jax
import jax.numpy as jnp
import numpy as np
from jax import lax
from jax.experimental import pallas as pl
from jax.experimental.pallas import tpu as pltpu
from jax.sharding import PartitionSpec as P

HEADS = 16
KV = 4
D = 128
AXES = ("head", "blk")
NEVER = 1 << 20
MASKED = -1e30
LOG2E_SCALE = float(np.log2(np.e) * D**-0.5)
VMEM_LIMIT = 32 * 1024 * 1024
SMALL_LIMIT = 8 * 1024 * 1024


def device_of(zl, x, y, zh, c):
    return ((zh % 4) * 2 + c % 2) * 32 + (zl % 2) * 16 + (x % 4) * 4 + y % 4


def place_of(device):
    h, b = device // 32, device % 32
    return b // 16, (b // 4) % 4, b % 4, h // 2, h % 2


def send(a, to):
    pairs = [(i, device_of(*to(*place_of(i)))) for i in range(256)]
    return lax.ppermute(a, AXES, pairs)


def along(first, step):
    def to(zl, x, y, zh, c):
        on_x = (c == 0) == first
        return (zl, x + step, y, zh, c) if on_x else (zl, x, y + step, zh, c)

    return to


SHIFTS = (0, 3, 1, 2)


def my_z():
    return lax.axis_index("head") // 2


def cut(arrays, s):
    head, at = lax.rem(my_z() + s, 4), 0
    for a in arrays:
        width = a.shape[1] // 4
        yield a, pl.ds(pl.multiple_of(head * width, width), width), at
        at += width


def pack_kernel(*refs):
    ins, outs, sems = refs[:3], refs[3:6], refs[6]
    copies = []
    for s, out in enumerate(outs):
        for i, (a, cols, at) in enumerate(cut(ins, s + 1)):
            width = a.shape[1] // 4
            copy = pltpu.make_async_copy(a.at[:, cols], out.at[:, pl.ds(at, width)], sems.at[s, i])
            copy.start()
            copies.append(copy)
    for copy in copies:
        copy.wait()


def pack(*arrays):
    width = sum(a.shape[1] for a in arrays) // 4
    vmem = pl.BlockSpec(memory_space=pltpu.VMEM)
    return pl.pallas_call(
        pack_kernel,
        out_shape=[jax.ShapeDtypeStruct((64, width), jnp.bfloat16)] * 3,
        in_specs=[pl.BlockSpec(memory_space=pl.ANY)] * 3,
        out_specs=[vmem] * 3,
        scratch_shapes=[pltpu.SemaphoreType.DMA((3, 3))],
        name="pack",
    )(*arrays)


def unpack_kernel(*refs):
    ins, outs = refs[:3], refs[6:]
    own = pl.ds(pl.multiple_of(my_z() * 64, 64), 64)
    for a, cols, at in cut(ins, 0):
        width = a.shape[1] // 4
        if at < 256:
            outs[0][own, pl.ds(at, width)] = a[:, cols]
        else:
            outs[1][own, :] = a[:, cols]
    for s in range(1, 4):
        rows = pl.ds(pl.multiple_of(lax.rem(my_z() + 4 - s, 4) * 64, 64), 64)
        outs[0][rows, :] = refs[2 + s][:, pl.ds(0, 256)]
        outs[1][rows, :] = refs[2 + s][:, pl.ds(256, 512)]


def unpack(arrays, got):
    vmem = pl.BlockSpec(memory_space=pltpu.VMEM)
    return pl.pallas_call(
        unpack_kernel,
        out_shape=[jax.ShapeDtypeStruct((256, w), jnp.bfloat16) for w in (256, 512)],
        in_specs=[vmem] * 6,
        out_specs=[vmem] * 2,
        compiler_params=pltpu.CompilerParams(vmem_limit_bytes=SMALL_LIMIT),
        name="unpack",
    )(*arrays, *got)


def finish_kernel(*refs):
    for s in range(4):
        z = lax.rem(my_z() + 4 - s, 4)
        refs[4][:, pl.ds(pl.multiple_of(z * 512, 512), 512)] = refs[s][...]


def finish(arrays):
    vmem = pl.BlockSpec(memory_space=pltpu.VMEM)
    return pl.pallas_call(
        finish_kernel,
        out_shape=jax.ShapeDtypeStruct((64, HEADS * D), jnp.bfloat16),
        in_specs=[vmem] * 4,
        out_specs=vmem,
        compiler_params=pltpu.CompilerParams(vmem_limit_bytes=SMALL_LIMIT),
        name="finish",
    )(*arrays)


def over_z(arrays):
    return [
        send(a, lambda zl, x, y, z, c, s=s: (zl, x, y, z + s, c)) for s, a in enumerate(arrays, 1)
    ]


CALLS = ((1, 0, 12, 1, False), (1, 12, 4, 1, True), (0, 0, 16, 24, False))
PLAN = 72
Q_AT = 2 * len(CALLS) * PLAN
CORE_AT = Q_AT + 4
EDGE_AT = Q_AT + 5


def doc_start(meta, at):
    start = jnp.zeros_like(at)
    for s in range(3):
        edge = meta[EDGE_AT + s]
        start = jnp.maximum(start, jnp.where(edge <= at, edge, 0))
    return start


def plan_kernel(pos_hbm, seg_hbm, plan, first_ref, pos_ref, seg_ref, sems):
    core, block = lax.rem(lax.axis_index("head"), 2), lax.axis_index("blk")
    runs = [
        pltpu.make_async_copy(pos_hbm.at[:, pl.ds(h * 256, 128)], first_ref.at[h], sems.at[h])
        for h in range(2)
    ]
    whole = [
        pltpu.make_async_copy(pos_hbm, pos_ref, sems.at[2]),
        pltpu.make_async_copy(seg_hbm, seg_ref, sems.at[3]),
    ]
    for copy in whole + runs:
        copy.start()
    for copy in whole:
        copy.wait()
    zl, x, y = block // 16, (block // 4) % 4, block % 4
    pos, seg = pos_ref[...], seg_ref[...]
    for s in range(1, 4):
        plan[EDGE_AT + s - 1] = jnp.min(jnp.where(seg >= s, pos, NEVER))
    plan[CORE_AT] = core
    for copy in runs:
        copy.wait()
    queries = []
    for whose in range(2):
        for hf in range(2):
            qb = first_ref[hf, (block + 16 * whose) % 32, 0]
            plan[Q_AT + whose * 2 + hf] = qb
            queries.append((qb, doc_start(plan, qb), doc_start(plan, qb + 255)))
    for call, (whose, first, blocks, _, carry) in enumerate(CALLS):
        counts = [[jnp.int32(0), jnp.int32(0)] for _ in range(2)]
        for k in range(first, first + blocks):
            s1, s2 = SHIFTS[k % 4], SHIFTS[k // 4]
            on_x, on_y = jnp.where(core == 0, s1, s2), jnp.where(core == 0, s2, s1)
            source = zl * 16 + (x + on_x) % 4 * 4 + (y + on_y) % 4
            for t in range(2):
                kb = first_ref[t, source, 0]
                entry = ((k - first) * 2 + t) + kb * 256
                for hf in range(2):
                    off = (call * 2 + hf) * PLAN
                    qb, lo_first, lo_last = queries[whose * 2 + hf]
                    n_full, n_part = counts[hf]
                    seen = (kb <= qb) & (kb + 255 >= lo_first)
                    whole = seen & (kb < qb) & (kb >= (lo_last if carry else lo_first))
                    plan[off + 2 + n_full] = entry
                    plan[off + 36 + n_part] = entry
                    counts[hf][0] = n_full + jnp.where(whole, 1, 0)
                    counts[hf][1] = n_part + jnp.where(seen & jnp.logical_not(whole), 1, 0)
        for hf in range(2):
            off = (call * 2 + hf) * PLAN
            n_full, n_part = counts[hf]
            odd = n_full % 2
            last = plan[off + 2 + jnp.maximum(n_full - 1, 0)]
            plan[off + 36 + n_part] = jnp.where(odd == 1, last, plan[off + 36 + n_part])
            plan[off] = n_full
            plan[off + 1] = n_part + odd


def make_plan(position, segment):
    return pl.pallas_call(
        plan_kernel,
        out_shape=jax.ShapeDtypeStruct((EDGE_AT + 3,), jnp.int32),
        in_specs=[pl.BlockSpec(memory_space=pl.ANY)] * 2,
        out_specs=pl.BlockSpec(memory_space=pltpu.SMEM),
        scratch_shapes=[
            pltpu.SMEM((2, 32, 128), jnp.int32),
            pltpu.VMEM((32, 512), jnp.int32),
            pltpu.VMEM((32, 512), jnp.int32),
            pltpu.SemaphoreType.DMA((4,)),
        ],
        compiler_params=pltpu.CompilerParams(vmem_limit_bytes=SMALL_LIMIT),
        name="plan",
    )(position, segment)


def three_parts(log_sum):
    lane = lax.broadcasted_iota(jnp.int32, log_sum.shape, 1)
    high = log_sum.astype(jnp.bfloat16).astype(jnp.float32)
    rest = log_sum - high
    mid = rest.astype(jnp.bfloat16).astype(jnp.float32)
    return jnp.where(lane < 4, high, jnp.where(lane < 8, mid, rest - mid)).astype(jnp.bfloat16)


def flash_kernel(pieces, call, carry, final, *refs):
    meta = refs[0]
    q_own, q_oth = refs[1], refs[2]
    piece_refs = refs[3 : 3 + len(pieces)]
    rest = list(refs[3 + len(pieces) :])
    if carry:
        acc_in, ml_in = rest.pop(0), rest.pop(0)
    out_a, out_b = rest.pop(0), rest.pop(0)
    kt, v_s, q_s, acc, m_s, l_s = rest
    if not final:
        acc = out_a
    core = meta[CORE_AT]

    tile = 0
    for piece, keys in zip(piece_refs, pieces):
        for t in range(keys // 128):
            rows = pl.ds(t * 128, 128)
            kt[tile] = piece[rows, pl.ds(0, D)].T
            v_s[tile] = piece[rows, pl.ds(D, D)]
            tile += 1

    for hf in range(2):
        for h in range(4):
            rows, cols = pl.ds(hf * 128, 128), pl.ds(h * 128, 128)
            q_s[hf * 4 + h, pl.ds(0, 128), :] = q_own[rows, cols]
            q_s[hf * 4 + h, pl.ds(128, 128), :] = q_oth[rows, cols]
            if carry:
                acc[hf * 4 + h] = acc_in[hf * 4 + h]
                m_s[hf * 4 + h] = jnp.broadcast_to(ml_in[hf, :, h : h + 1], (256, 128))
                lane = lax.broadcasted_iota(jnp.int32, (256, 128), 1)
                l_s[hf * 4 + h] = jnp.where(lane == 0, ml_in[hf, :, 4 + h : 5 + h], 0.0)
            else:
                acc[hf * 4 + h] = jnp.zeros((256, 128), jnp.float32)
                m_s[hf * 4 + h] = jnp.full((256, 128), MASKED, jnp.float32)
                l_s[hf * 4 + h] = jnp.zeros((256, 128), jnp.float32)

    row = lax.broadcasted_iota(jnp.int32, (256, 128), 0)
    lane = lax.broadcasted_iota(jnp.int32, (256, 128), 1)
    own_row = row < 128
    in_half = jnp.where(own_row, row, row - 128)
    q_core = jnp.where(own_row, core, 1 - core)
    q_off = jnp.where(in_half >= 64, in_half + 64, in_half) + q_core * 64
    k_off = jnp.where(lane >= 64, lane + 64, lane) + core * 64

    def step(hf, tile_a, tile_b, masks):
        k = jnp.concatenate([kt[tile_a], kt[tile_b]], 1)
        v = jnp.concatenate([v_s[tile_a], v_s[tile_b]], 0)
        ss = [
            lax.dot_general(
                q_s[hf * 4 + h], k, (((1,), (0,)), ((), ())), preferred_element_type=jnp.float32
            )
            for h in range(4)
        ]
        ps, fades = [], []
        for h in range(4):
            i = hf * 4 + h
            s_a, s_b = ss[h][:, :128], ss[h][:, 128:]
            if masks is not None:
                s_a = jnp.where(masks[0], s_a, MASKED)
                s_b = jnp.where(masks[1], s_b, MASKED)
            old = m_s[i]
            new = jnp.maximum(old, jnp.max(jnp.maximum(s_a, s_b), axis=1, keepdims=True))
            m_s[i] = new
            p_a = jnp.exp2((s_a - new) * LOG2E_SCALE)
            p_b = jnp.exp2((s_b - new) * LOG2E_SCALE)
            fades.append(jnp.exp2((old - new) * LOG2E_SCALE))
            l_s[i] = l_s[i] * fades[-1] + p_a + p_b
            ps.append(jnp.concatenate([p_a.astype(jnp.bfloat16), p_b.astype(jnp.bfloat16)], 1))
        for h in range(4):
            i = hf * 4 + h
            acc[i] = acc[i] * fades[h] + jnp.dot(ps[h], v, preferred_element_type=jnp.float32)

    def quad(hf, tiles4):
        k = jnp.concatenate([kt[t] for t in tiles4], 1)
        v = jnp.concatenate([v_s[t] for t in tiles4], 0)
        ss = [
            lax.dot_general(
                q_s[hf * 4 + h], k, (((1,), (0,)), ((), ())), preferred_element_type=jnp.float32
            )
            for h in range(4)
        ]
        ps, fades = [], []
        for h in range(4):
            i = hf * 4 + h
            st = [ss[h][:, t * 128 : t * 128 + 128] for t in range(4)]
            top = jnp.maximum(jnp.maximum(st[0], st[1]), jnp.maximum(st[2], st[3]))
            old = m_s[i]
            new = jnp.maximum(old, jnp.max(top, axis=1, keepdims=True))
            m_s[i] = new
            p = [jnp.exp2((a - new) * LOG2E_SCALE) for a in st]
            fades.append(jnp.exp2((old - new) * LOG2E_SCALE))
            l_s[i] = l_s[i] * fades[-1] + (p[0] + p[1]) + (p[2] + p[3])
            ps.append(jnp.concatenate([a.astype(jnp.bfloat16) for a in p], 1))
        for h in range(4):
            i = hf * 4 + h
            acc[i] = acc[i] * fades[h] + jnp.dot(ps[h], v, preferred_element_type=jnp.float32)

    for hf in range(2):
        qb = meta[Q_AT + CALLS[call][0] * 2 + hf]
        off = (call * 2 + hf) * PLAN
        n_full, n_part = meta[off], meta[off + 1]

        def whole(j):
            return meta[off + 2 + j] & 255

        def whole_quad(j, _):
            quad(hf, [whole(4 * j + t) for t in range(4)])
            return 0

        lax.fori_loop(0, n_full // 4, whole_quad, 0)

        def whole_pair(j, _):
            step(hf, whole(2 * j), whole(2 * j + 1), None)
            return 0

        lax.fori_loop(n_full // 4 * 2, n_full // 2, whole_pair, 0)

        q_pos = qb + q_off
        q_lo = doc_start(meta, q_pos)
        if not carry:

            @pl.when(doc_start(meta, qb + 255) > doc_start(meta, qb))
            def forget():
                keep = q_lo <= qb
                for h in range(4):
                    i = hf * 4 + h
                    m_s[i] = jnp.where(keep, m_s[i], MASKED)
                    l_s[i] = jnp.where(keep, l_s[i], 0.0)
                    acc[i] = jnp.where(keep, acc[i], 0.0)

        def part_pair(j, _):
            there = 2 * j + 1 < n_part
            e_a = meta[off + 36 + 2 * j]
            e_b = jnp.where(there, meta[off + 37 + 2 * j], e_a)
            tile_a, tile_b = e_a & 255, e_b & 255
            k_a = (e_a >> 8) + k_off
            k_b = jnp.where(there, e_b >> 8, NEVER) + k_off
            masks = ((k_a <= q_pos) & (k_a >= q_lo), (k_b <= q_pos) & (k_b >= q_lo))
            step(hf, tile_a, tile_b, masks)
            return 0

        lax.fori_loop(0, (n_part + 1) // 2, part_pair, 0)

        stats = jnp.zeros((256, 128), jnp.float32)
        rows = pl.ds(hf * 128, 128)
        for h in range(4):
            i, cols = hf * 4 + h, pl.ds(h * 128, 128)
            total = jnp.sum(l_s[i], axis=1, keepdims=True)
            if final:
                total = jnp.maximum(total, 1e-30)
                log_sum = m_s[i] * LOG2E_SCALE + jnp.log2(total)
                stats = jnp.where((lane % 4 == h) & (lane < 12), log_sum, stats)
                mean = acc[i] * (1 / total)
                out_a[rows, cols] = mean[:128]
                out_b[rows, cols] = mean[128:].astype(jnp.bfloat16)
            else:
                stats = jnp.where(lane == h, m_s[i], stats)
                stats = jnp.where(lane == 4 + h, total, stats)
        if final:
            out_a[rows, pl.ds(512, 128)] = stats[:128]
            out_b[rows, pl.ds(512, 128)] = three_parts(stats[128:])
        else:
            out_b[hf] = stats


def flash(meta, q_own, q_oth, pieces, call, state, final):
    rows = tuple(p.shape[0] for p in pieces)
    carry = state is not None
    keys = sum(rows)
    if final:
        shapes = [jax.ShapeDtypeStruct((256, 640), t) for t in (jnp.float32, jnp.bfloat16)]
    else:
        shapes = [
            jax.ShapeDtypeStruct((8, 256, 128), jnp.float32),
            jax.ShapeDtypeStruct((2, 256, 128), jnp.float32),
        ]
    vmem = pl.BlockSpec(memory_space=pltpu.VMEM)
    in_specs = [pl.BlockSpec(memory_space=pltpu.SMEM), vmem, vmem]
    in_specs += [vmem] * (len(pieces) + (2 if carry else 0))
    return pl.pallas_call(
        functools.partial(flash_kernel, rows, call, carry, final),
        out_shape=shapes,
        in_specs=in_specs,
        out_specs=[vmem, vmem],
        scratch_shapes=[
            pltpu.VMEM((keys // 128, 128, 128), jnp.bfloat16),
            pltpu.VMEM((keys // 128, 128, 128), jnp.bfloat16),
            pltpu.VMEM((8, 256, 128), jnp.bfloat16),
            pltpu.VMEM((8 if final else 1, 256, 128), jnp.float32),
            pltpu.VMEM((8, 256, 128), jnp.float32),
            pltpu.VMEM((8, 256, 128), jnp.float32),
        ],
        compiler_params=pltpu.CompilerParams(vmem_limit_bytes=VMEM_LIMIT),
        cost_estimate=pl.CostEstimate(
            flops=CALLS[call][3] * 2048 * keys * D, bytes_accessed=keys * 512, transcendentals=0
        ),
        name="flash",
    )(meta, q_own, q_oth, *pieces, *(state if carry else ()))


def merge_kernel(count, *refs):
    ins, outs = refs[:count], refs[count:]
    step = 256 // len(outs)
    for s, out in enumerate(outs):
        at = lax.rem(my_z() + s, 4) * 64 if len(outs) == 4 else 0
        rows = pl.ds(pl.multiple_of(at, 64), step)
        logs = []
        for a in ins:
            log_sum = a[rows, pl.ds(512, 128)].astype(jnp.float32)
            if a.dtype == jnp.bfloat16:
                log_sum = log_sum[:, 0:4] + log_sum[:, 4:8] + log_sum[:, 8:12]
            logs.append(log_sum[:, 0:4])
        top = functools.reduce(jnp.maximum, logs)
        weights = [jnp.exp2(log_sum - top) for log_sum in logs]
        total = sum(weights)
        weights = [w / total for w in weights]
        for h in range(4):
            cols = pl.ds(h * 128, 128)
            mixed = sum(
                a[rows, cols].astype(jnp.float32) * w[:, h : h + 1] for a, w in zip(ins, weights)
            )
            out[:, cols] = mixed.astype(jnp.bfloat16)
        if len(outs) == 1:
            log_sum = top + jnp.log2(total)
            lane = lax.broadcasted_iota(jnp.int32, (step, 128), 1)
            spread = jnp.zeros((step, 128), jnp.float32)
            for h in range(4):
                spread = jnp.where((lane % 4 == h) & (lane < 12), log_sum[:, h : h + 1], spread)
            out[:, pl.ds(512, 128)] = three_parts(spread)


def merge(partials, last):
    vmem = pl.BlockSpec(memory_space=pltpu.VMEM)
    shape, count = ((64, 512), 4) if last else ((256, 640), 1)
    return pl.pallas_call(
        functools.partial(merge_kernel, len(partials)),
        out_shape=[jax.ShapeDtypeStruct(shape, jnp.bfloat16)] * count,
        in_specs=[vmem] * len(partials),
        out_specs=[vmem] * count,
        compiler_params=pltpu.CompilerParams(vmem_limit_bytes=SMALL_LIMIT),
        name="merge",
    )(*partials)


def other_core(zl, x, y, zh, c):
    return (zl, x, y, zh, c + 1)


def other_lo(zl, x, y, zh, c):
    return (zl + 1, x, y, zh, c)


def after(first, *then):
    return lax.optimization_barrier((first, *then))[1:]


def local(queries, keys, values, position, segment):
    with jax.named_scope("heads"):
        held = keys.reshape(64, 512), values.reshape(64, 512), queries.reshape(64, 2048)
        plan = make_plan(position, segment)
        kv, q_own = unpack(held, after(plan, *over_z(pack(*held))))
    with jax.named_scope("kv_first"):
        line = [kv] + [send(kv, along(True, step)) for step in (1, -1, 2)]
        line_a, line_b = jnp.concatenate(line[:2], 0), jnp.concatenate(line[2:], 0)
    with jax.named_scope("kv_second"):
        up_a, down_b = send(line_a, along(False, 1)), send(line_b, along(False, -1))
        up_b, down_a = send(line_b, along(False, 1)), send(line_a, along(False, -1))
        far_a, far_b = send(up_a, along(False, 1)), send(down_b, along(False, -1))
    with jax.named_scope("q_other"):
        q_oth = send(*after(line_a, q_own), other_core)
        far_own = send(q_own, other_lo)
        (far_own,) = after(up_b, far_own)
        far_oth = send(far_own, other_core)
    with jax.named_scope("attend_far"):
        keys = [line_a, line_b, up_a, up_b, down_a, down_b, far_a, far_b]
        state = flash(plan, far_own, far_oth, keys[:6], 0, None, False)
        mine, theirs = flash(plan, far_own, far_oth, keys[6:], 1, state, True)
    with jax.named_scope("merge_far"):
        (far,) = merge([mine, send(theirs, other_core)], False)
        far_got = send(far, other_lo)
    with jax.named_scope("attend_own"):
        q_own, q_oth = after(far, q_own, q_oth)
        mine, theirs = flash(plan, q_own, q_oth, keys, 2, None, True)
    with jax.named_scope("merge_own"):
        (theirs,) = after(far_got, theirs)
        parts = merge([mine, send(theirs, other_core), far_got], True)
    with jax.named_scope("out_heads"):
        out = finish([parts[0]] + over_z(parts[1:]))
    return out.reshape(1, 64, HEADS * D)


def solution(mesh):
    spec = P("blk", "head", None)
    return jax.shard_map(
        local,
        mesh=mesh,
        in_specs=(spec, spec, spec, P(), P()),
        out_specs=spec,
        check_vma=False,
    )
```

```python
import functools

import jax
import jax.numpy as jnp
import numpy as np
from jax import lax
from jax.experimental import pallas as pl
from jax.experimental.pallas import tpu as pltpu
from jax.sharding import PartitionSpec as P

HEADS = 16
KV = 4
D = 128
AXES = ("head", "blk")
NEVER = 1 << 20
MASKED = -1e30
LOG2E_SCALE = float(np.log2(np.e) * D**-0.5)
VMEM_LIMIT = 32 * 1024 * 1024
SMALL_LIMIT = 8 * 1024 * 1024


def device_of(zl, x, y, zh, c):
    return ((zh % 4) * 2 + c % 2) * 32 + (zl % 2) * 16 + (x % 4) * 4 + y % 4


def place_of(device):
    h, b = device // 32, device % 32
    return b // 16, (b // 4) % 4, b % 4, h // 2, h % 2


def send(a, to):
    pairs = [(i, device_of(*to(*place_of(i)))) for i in range(256)]
    return lax.ppermute(a, AXES, pairs)


def along(first, step):
    def to(zl, x, y, zh, c):
        on_x = (c == 0) == first
        return (zl, x + step, y, zh, c) if on_x else (zl, x, y + step, zh, c)

    return to


SHIFTS = (0, 3, 1, 2)


def my_z():
    return lax.axis_index("head") // 2


def cut(arrays, s):
    head, at = lax.rem(my_z() + s, 4), 0
    for a in arrays:
        width = a.shape[1] // 4
        yield a, pl.ds(pl.multiple_of(head * width, width), width), at
        at += width


def pack_kernel(*refs):
    ins, outs, sems = refs[:3], refs[3:6], refs[6]
    copies = []
    for s, out in enumerate(outs):
        for i, (a, cols, at) in enumerate(cut(ins, s + 1)):
            width = a.shape[1] // 4
            copy = pltpu.make_async_copy(a.at[:, cols], out.at[:, pl.ds(at, width)], sems.at[s, i])
            copy.start()
            copies.append(copy)
    for copy in copies:
        copy.wait()


def pack(*arrays):
    width = sum(a.shape[1] for a in arrays) // 4
    vmem = pl.BlockSpec(memory_space=pltpu.VMEM)
    return pl.pallas_call(
        pack_kernel,
        out_shape=[jax.ShapeDtypeStruct((64, width), jnp.bfloat16)] * 3,
        in_specs=[pl.BlockSpec(memory_space=pl.ANY)] * 3,
        out_specs=[vmem] * 3,
        scratch_shapes=[pltpu.SemaphoreType.DMA((3, 3))],
        name="pack",
    )(*arrays)


def unpack_kernel(*refs):
    ins, outs = refs[:3], refs[6:]
    own = pl.ds(pl.multiple_of(my_z() * 64, 64), 64)
    for a, cols, at in cut(ins, 0):
        width = a.shape[1] // 4
        if at < 256:
            outs[0][own, pl.ds(at, width)] = a[:, cols]
        else:
            outs[1][own, :] = a[:, cols]
    for s in range(1, 4):
        rows = pl.ds(pl.multiple_of(lax.rem(my_z() + 4 - s, 4) * 64, 64), 64)
        outs[0][rows, :] = refs[2 + s][:, pl.ds(0, 256)]
        outs[1][rows, :] = refs[2 + s][:, pl.ds(256, 512)]


def unpack(arrays, got):
    vmem = pl.BlockSpec(memory_space=pltpu.VMEM)
    return pl.pallas_call(
        unpack_kernel,
        out_shape=[jax.ShapeDtypeStruct((256, w), jnp.bfloat16) for w in (256, 512)],
        in_specs=[vmem] * 6,
        out_specs=[vmem] * 2,
        compiler_params=pltpu.CompilerParams(vmem_limit_bytes=SMALL_LIMIT),
        name="unpack",
    )(*arrays, *got)


def finish_kernel(*refs):
    for s in range(4):
        z = lax.rem(my_z() + 4 - s, 4)
        refs[4][:, pl.ds(pl.multiple_of(z * 512, 512), 512)] = refs[s][...]


def finish(arrays):
    vmem = pl.BlockSpec(memory_space=pltpu.VMEM)
    return pl.pallas_call(
        finish_kernel,
        out_shape=jax.ShapeDtypeStruct((64, HEADS * D), jnp.bfloat16),
        in_specs=[vmem] * 4,
        out_specs=vmem,
        compiler_params=pltpu.CompilerParams(vmem_limit_bytes=SMALL_LIMIT),
        name="finish",
    )(*arrays)


def over_z(arrays):
    got = {}
    for s in (2, 1, 3):
        got[s] = send(arrays[s - 1], lambda zl, x, y, z, c, s=s: (zl, x, y, z + s, c))
    return [got[s] for s in (1, 2, 3)]


CALLS = ((1, 0, 12, 1, False), (1, 12, 4, 1, True), (0, 0, 16, 24, False))
PLAN = 72
Q_AT = 2 * len(CALLS) * PLAN
CORE_AT = Q_AT + 4
EDGE_AT = Q_AT + 5


def doc_start(meta, at):
    start = jnp.zeros_like(at)
    for s in range(3):
        edge = meta[EDGE_AT + s]
        start = jnp.maximum(start, jnp.where(edge <= at, edge, 0))
    return start


def plan_kernel(pos_hbm, seg_hbm, plan, first_ref, pos_ref, seg_ref, sems):
    core, block = lax.rem(lax.axis_index("head"), 2), lax.axis_index("blk")
    runs = [
        pltpu.make_async_copy(pos_hbm.at[:, pl.ds(h * 256, 128)], first_ref.at[h], sems.at[h])
        for h in range(2)
    ]
    whole = [
        pltpu.make_async_copy(pos_hbm, pos_ref, sems.at[2]),
        pltpu.make_async_copy(seg_hbm, seg_ref, sems.at[3]),
    ]
    for copy in whole + runs:
        copy.start()
    for copy in whole:
        copy.wait()
    zl, x, y = block // 16, (block // 4) % 4, block % 4
    pos, seg = pos_ref[...], seg_ref[...]
    for s in range(1, 4):
        plan[EDGE_AT + s - 1] = jnp.min(jnp.where(seg >= s, pos, NEVER))
    plan[CORE_AT] = core
    for copy in runs:
        copy.wait()
    queries = []
    for whose in range(2):
        for hf in range(2):
            qb = first_ref[hf, (block + 16 * whose) % 32, 0]
            plan[Q_AT + whose * 2 + hf] = qb
            queries.append((qb, doc_start(plan, qb), doc_start(plan, qb + 255)))
    for call, (whose, first, blocks, _, carry) in enumerate(CALLS):
        counts = [[jnp.int32(0), jnp.int32(0)] for _ in range(2)]
        for k in range(first, first + blocks):
            s1, s2 = SHIFTS[k % 4], SHIFTS[k // 4]
            on_x, on_y = jnp.where(core == 0, s1, s2), jnp.where(core == 0, s2, s1)
            source = zl * 16 + (x + on_x) % 4 * 4 + (y + on_y) % 4
            for t in range(2):
                kb = first_ref[t, source, 0]
                entry = ((k - first) * 2 + t) + kb * 256
                for hf in range(2):
                    off = (call * 2 + hf) * PLAN
                    qb, lo_first, lo_last = queries[whose * 2 + hf]
                    n_full, n_part = counts[hf]
                    seen = (kb <= qb) & (kb + 255 >= lo_first)
                    whole = seen & (kb < qb) & (kb >= (lo_last if carry else lo_first))
                    plan[off + 2 + n_full] = entry
                    plan[off + 36 + n_part] = entry
                    counts[hf][0] = n_full + jnp.where(whole, 1, 0)
                    counts[hf][1] = n_part + jnp.where(seen & jnp.logical_not(whole), 1, 0)
        for hf in range(2):
            off = (call * 2 + hf) * PLAN
            n_full, n_part = counts[hf]
            odd = n_full % 2
            last = plan[off + 2 + jnp.maximum(n_full - 1, 0)]
            plan[off + 36 + n_part] = jnp.where(odd == 1, last, plan[off + 36 + n_part])
            plan[off] = n_full
            plan[off + 1] = n_part + odd


def make_plan(position, segment):
    return pl.pallas_call(
        plan_kernel,
        out_shape=jax.ShapeDtypeStruct((EDGE_AT + 3,), jnp.int32),
        in_specs=[pl.BlockSpec(memory_space=pl.ANY)] * 2,
        out_specs=pl.BlockSpec(memory_space=pltpu.SMEM),
        scratch_shapes=[
            pltpu.SMEM((2, 32, 128), jnp.int32),
            pltpu.VMEM((32, 512), jnp.int32),
            pltpu.VMEM((32, 512), jnp.int32),
            pltpu.SemaphoreType.DMA((4,)),
        ],
        compiler_params=pltpu.CompilerParams(vmem_limit_bytes=SMALL_LIMIT),
        name="plan",
    )(position, segment)


def three_parts(log_sum):
    lane = lax.broadcasted_iota(jnp.int32, log_sum.shape, 1)
    high = log_sum.astype(jnp.bfloat16).astype(jnp.float32)
    rest = log_sum - high
    mid = rest.astype(jnp.bfloat16).astype(jnp.float32)
    return jnp.where(lane < 4, high, jnp.where(lane < 8, mid, rest - mid)).astype(jnp.bfloat16)


def flash_kernel(pieces, call, carry, final, *refs):
    meta = refs[0]
    q_own, q_oth = refs[1], refs[2]
    piece_refs = refs[3 : 3 + len(pieces)]
    rest = list(refs[3 + len(pieces) :])
    if carry:
        acc_in, ml_in = rest.pop(0), rest.pop(0)
    out_a, out_b = rest.pop(0), rest.pop(0)
    kt, v_s, q_s, acc, m_s, l_s = rest
    if not final:
        acc = out_a
    core = meta[CORE_AT]

    tile = 0
    for piece, keys in zip(piece_refs, pieces):
        for t in range(keys // 128):
            rows = pl.ds(t * 128, 128)
            kt[tile] = piece[rows, pl.ds(0, D)].T
            v_s[tile] = piece[rows, pl.ds(D, D)]
            tile += 1

    for hf in range(2):
        for h in range(4):
            rows, cols = pl.ds(hf * 128, 128), pl.ds(h * 128, 128)
            q_s[hf * 4 + h, pl.ds(0, 128), :] = q_own[rows, cols]
            q_s[hf * 4 + h, pl.ds(128, 128), :] = q_oth[rows, cols]
            if carry:
                acc[hf * 4 + h] = acc_in[hf * 4 + h]
                m_s[hf * 4 + h] = jnp.broadcast_to(ml_in[hf, :, h : h + 1], (256, 128))
                lane = lax.broadcasted_iota(jnp.int32, (256, 128), 1)
                l_s[hf * 4 + h] = jnp.where(lane == 0, ml_in[hf, :, 4 + h : 5 + h], 0.0)
            else:
                acc[hf * 4 + h] = jnp.zeros((256, 128), jnp.float32)
                m_s[hf * 4 + h] = jnp.full((256, 128), MASKED, jnp.float32)
                l_s[hf * 4 + h] = jnp.zeros((256, 128), jnp.float32)

    row = lax.broadcasted_iota(jnp.int32, (256, 128), 0)
    lane = lax.broadcasted_iota(jnp.int32, (256, 128), 1)
    own_row = row < 128
    in_half = jnp.where(own_row, row, row - 128)
    q_core = jnp.where(own_row, core, 1 - core)
    q_off = jnp.where(in_half >= 64, in_half + 64, in_half) + q_core * 64
    k_off = jnp.where(lane >= 64, lane + 64, lane) + core * 64

    def step(hf, tile_a, tile_b, masks):
        k = jnp.concatenate([kt[tile_a], kt[tile_b]], 1)
        v = jnp.concatenate([v_s[tile_a], v_s[tile_b]], 0)
        ss = [
            lax.dot_general(
                q_s[hf * 4 + h], k, (((1,), (0,)), ((), ())), preferred_element_type=jnp.float32
            )
            for h in range(4)
        ]
        ps, fades = [], []
        for h in range(4):
            i = hf * 4 + h
            s_a, s_b = ss[h][:, :128], ss[h][:, 128:]
            if masks is not None:
                s_a = jnp.where(masks[0], s_a, MASKED)
                s_b = jnp.where(masks[1], s_b, MASKED)
            old = m_s[i]
            new = jnp.maximum(old, jnp.max(jnp.maximum(s_a, s_b), axis=1, keepdims=True))
            m_s[i] = new
            p_a = jnp.exp2((s_a - new) * LOG2E_SCALE)
            p_b = jnp.exp2((s_b - new) * LOG2E_SCALE)
            fades.append(jnp.exp2((old - new) * LOG2E_SCALE))
            l_s[i] = l_s[i] * fades[-1] + p_a + p_b
            ps.append(jnp.concatenate([p_a.astype(jnp.bfloat16), p_b.astype(jnp.bfloat16)], 1))
        for h in range(4):
            i = hf * 4 + h
            acc[i] = acc[i] * fades[h] + jnp.dot(ps[h], v, preferred_element_type=jnp.float32)

    def quad(hf, tiles4):
        k = jnp.concatenate([kt[t] for t in tiles4], 1)
        v = jnp.concatenate([v_s[t] for t in tiles4], 0)
        ss = [
            lax.dot_general(
                q_s[hf * 4 + h], k, (((1,), (0,)), ((), ())), preferred_element_type=jnp.float32
            )
            for h in range(4)
        ]
        ps, fades = [], []
        for h in range(4):
            i = hf * 4 + h
            st = [ss[h][:, t * 128 : t * 128 + 128] for t in range(4)]
            top = jnp.maximum(jnp.maximum(st[0], st[1]), jnp.maximum(st[2], st[3]))
            old = m_s[i]
            new = jnp.maximum(old, jnp.max(top, axis=1, keepdims=True))
            m_s[i] = new
            p = [jnp.exp2((a - new) * LOG2E_SCALE) for a in st]
            fades.append(jnp.exp2((old - new) * LOG2E_SCALE))
            l_s[i] = l_s[i] * fades[-1] + (p[0] + p[1]) + (p[2] + p[3])
            ps.append(jnp.concatenate([a.astype(jnp.bfloat16) for a in p], 1))
        for h in range(4):
            i = hf * 4 + h
            acc[i] = acc[i] * fades[h] + jnp.dot(ps[h], v, preferred_element_type=jnp.float32)

    for hf in range(2):
        qb = meta[Q_AT + CALLS[call][0] * 2 + hf]
        off = (call * 2 + hf) * PLAN
        n_full, n_part = meta[off], meta[off + 1]

        def whole(j):
            return meta[off + 2 + j] & 255

        def whole_quad(j, _):
            quad(hf, [whole(4 * j + t) for t in range(4)])
            return 0

        lax.fori_loop(0, n_full // 4, whole_quad, 0)

        def whole_pair(j, _):
            step(hf, whole(2 * j), whole(2 * j + 1), None)
            return 0

        lax.fori_loop(n_full // 4 * 2, n_full // 2, whole_pair, 0)

        q_pos = qb + q_off
        q_lo = doc_start(meta, q_pos)
        if not carry:

            @pl.when(doc_start(meta, qb + 255) > doc_start(meta, qb))
            def forget():
                keep = q_lo <= qb
                for h in range(4):
                    i = hf * 4 + h
                    m_s[i] = jnp.where(keep, m_s[i], MASKED)
                    l_s[i] = jnp.where(keep, l_s[i], 0.0)
                    acc[i] = jnp.where(keep, acc[i], 0.0)

        def part_pair(j, _):
            there = 2 * j + 1 < n_part
            e_a = meta[off + 36 + 2 * j]
            e_b = jnp.where(there, meta[off + 37 + 2 * j], e_a)
            tile_a, tile_b = e_a & 255, e_b & 255
            k_a = (e_a >> 8) + k_off
            k_b = jnp.where(there, e_b >> 8, NEVER) + k_off
            masks = ((k_a <= q_pos) & (k_a >= q_lo), (k_b <= q_pos) & (k_b >= q_lo))
            step(hf, tile_a, tile_b, masks)
            return 0

        lax.fori_loop(0, (n_part + 1) // 2, part_pair, 0)

        stats = jnp.zeros((256, 128), jnp.float32)
        rows = pl.ds(hf * 128, 128)
        for h in range(4):
            i, cols = hf * 4 + h, pl.ds(h * 128, 128)
            total = jnp.sum(l_s[i], axis=1, keepdims=True)
            if final:
                total = jnp.maximum(total, 1e-30)
                log_sum = m_s[i] * LOG2E_SCALE + jnp.log2(total)
                stats = jnp.where((lane % 4 == h) & (lane < 12), log_sum, stats)
                mean = acc[i] * (1 / total)
                out_a[rows, cols] = mean[:128]
                out_b[rows, cols] = mean[128:].astype(jnp.bfloat16)
            else:
                stats = jnp.where(lane == h, m_s[i], stats)
                stats = jnp.where(lane == 4 + h, total, stats)
        if final:
            out_a[rows, pl.ds(512, 128)] = stats[:128]
            out_b[rows, pl.ds(512, 128)] = three_parts(stats[128:])
        else:
            out_b[hf] = stats


def flash(meta, q_own, q_oth, pieces, call, state, final):
    rows = tuple(p.shape[0] for p in pieces)
    carry = state is not None
    keys = sum(rows)
    if final:
        shapes = [jax.ShapeDtypeStruct((256, 640), t) for t in (jnp.float32, jnp.bfloat16)]
    else:
        shapes = [
            jax.ShapeDtypeStruct((8, 256, 128), jnp.float32),
            jax.ShapeDtypeStruct((2, 256, 128), jnp.float32),
        ]
    vmem = pl.BlockSpec(memory_space=pltpu.VMEM)
    in_specs = [pl.BlockSpec(memory_space=pltpu.SMEM), vmem, vmem]
    in_specs += [vmem] * (len(pieces) + (2 if carry else 0))
    return pl.pallas_call(
        functools.partial(flash_kernel, rows, call, carry, final),
        out_shape=shapes,
        in_specs=in_specs,
        out_specs=[vmem, vmem],
        scratch_shapes=[
            pltpu.VMEM((keys // 128, 128, 128), jnp.bfloat16),
            pltpu.VMEM((keys // 128, 128, 128), jnp.bfloat16),
            pltpu.VMEM((8, 256, 128), jnp.bfloat16),
            pltpu.VMEM((8 if final else 1, 256, 128), jnp.float32),
            pltpu.VMEM((8, 256, 128), jnp.float32),
            pltpu.VMEM((8, 256, 128), jnp.float32),
        ],
        compiler_params=pltpu.CompilerParams(vmem_limit_bytes=VMEM_LIMIT),
        cost_estimate=pl.CostEstimate(
            flops=CALLS[call][3] * 2048 * keys * D, bytes_accessed=keys * 512, transcendentals=0
        ),
        name="flash",
    )(meta, q_own, q_oth, *pieces, *(state if carry else ()))


def merge_kernel(count, *refs):
    ins, outs = refs[:count], refs[count:]
    step = 256 // len(outs)
    for s, out in enumerate(outs):
        at = lax.rem(my_z() + s, 4) * 64 if len(outs) == 4 else 0
        rows = pl.ds(pl.multiple_of(at, 64), step)
        logs = []
        for a in ins:
            log_sum = a[rows, pl.ds(512, 128)].astype(jnp.float32)
            if a.dtype == jnp.bfloat16:
                log_sum = log_sum[:, 0:4] + log_sum[:, 4:8] + log_sum[:, 8:12]
            logs.append(log_sum[:, 0:4])
        top = functools.reduce(jnp.maximum, logs)
        weights = [jnp.exp2(log_sum - top) for log_sum in logs]
        total = sum(weights)
        weights = [w / total for w in weights]
        for h in range(4):
            cols = pl.ds(h * 128, 128)
            mixed = sum(
                a[rows, cols].astype(jnp.float32) * w[:, h : h + 1] for a, w in zip(ins, weights)
            )
            out[:, cols] = mixed.astype(jnp.bfloat16)
        if len(outs) == 1:
            log_sum = top + jnp.log2(total)
            lane = lax.broadcasted_iota(jnp.int32, (step, 128), 1)
            spread = jnp.zeros((step, 128), jnp.float32)
            for h in range(4):
                spread = jnp.where((lane % 4 == h) & (lane < 12), log_sum[:, h : h + 1], spread)
            out[:, pl.ds(512, 128)] = three_parts(spread)


def merge(partials, last):
    vmem = pl.BlockSpec(memory_space=pltpu.VMEM)
    shape, count = ((64, 512), 4) if last else ((256, 640), 1)
    return pl.pallas_call(
        functools.partial(merge_kernel, len(partials)),
        out_shape=[jax.ShapeDtypeStruct(shape, jnp.bfloat16)] * count,
        in_specs=[vmem] * len(partials),
        out_specs=[vmem] * count,
        compiler_params=pltpu.CompilerParams(vmem_limit_bytes=SMALL_LIMIT),
        name="merge",
    )(*partials)


def other_core(zl, x, y, zh, c):
    return (zl, x, y, zh, c + 1)


def other_lo(zl, x, y, zh, c):
    return (zl + 1, x, y, zh, c)


def after(first, *then):
    return lax.optimization_barrier((first, *then))[1:]


def local(queries, keys, values, position, segment):
    with jax.named_scope("heads"):
        held = keys.reshape(64, 512), values.reshape(64, 512), queries.reshape(64, 2048)
        plan = make_plan(position, segment)
        kv, q_own = unpack(held, after(plan, *over_z(pack(*held))))
    with jax.named_scope("kv_first"):
        line = [kv] + [send(kv, along(True, step)) for step in (1, -1, 2)]
        line_a, line_b = jnp.concatenate(line[:2], 0), jnp.concatenate(line[2:], 0)
    with jax.named_scope("kv_second"):
        up_a, down_b = send(line_a, along(False, 1)), send(line_b, along(False, -1))
        up_b, down_a = send(line_b, along(False, 1)), send(line_a, along(False, -1))
        far_a, far_b = send(up_a, along(False, 1)), send(down_b, along(False, -1))
    with jax.named_scope("q_other"):
        q_oth = send(*after(line_a, q_own), other_core)
        far_own = send(q_own, other_lo)
        (far_own,) = after(up_b, far_own)
        far_oth = send(far_own, other_core)
    with jax.named_scope("attend_far"):
        keys = [line_a, line_b, up_a, up_b, down_a, down_b, far_a, far_b]
        state = flash(plan, far_own, far_oth, keys[:6], 0, None, False)
        mine, theirs = flash(plan, far_own, far_oth, keys[6:], 1, state, True)
    with jax.named_scope("merge_far"):
        (far,) = merge([mine, send(theirs, other_core)], False)
        far_got = send(far, other_lo)
    with jax.named_scope("attend_own"):
        q_own, q_oth = after(far, q_own, q_oth)
        mine, theirs = flash(plan, q_own, q_oth, keys, 2, None, True)
    with jax.named_scope("merge_own"):
        (theirs,) = after(far_got, theirs)
        parts = merge([mine, send(theirs, other_core), far_got], True)
    with jax.named_scope("out_heads"):
        out = finish([parts[0]] + over_z(parts[1:]))
    return out.reshape(1, 64, HEADS * D)


def solution(mesh):
    spec = P("blk", "head", None)
    return jax.shard_map(
        local,
        mesh=mesh,
        in_specs=(spec, spec, spec, P(), P()),
        out_specs=spec,
        check_vma=False,
    )
```
